512 devices in a mesh: feat: 32 (over x, y, core), dp: 16 (over z).
Axes of the slice: x: 4, y: 4, z: 16, core: 2. Of those that a mesh axis runs over, the one named last changes fastest.
Arguments:
- feature_table: bfloat16 [65536, 256], P('feat'), may hold values from -6 to 6
- row_state: float32 [65536], P('feat'), may hold values from 0.01 to 1
- rel_diag: bfloat16 [4096, 256], replicated, may hold values from -103 to 103
- slot_rows: int32 [512, 32, 128], P(('feat', 'dp')), may hold values from 0 to 2047
- slot_counts: int32 [512, 32], P(('feat', 'dp')), may hold values from 1 to 128, as said below
- head_bags: int32 [131072, 16], P(('feat', 'dp')), may hold values from 0 to 4095, as said below
- tail_bags: int32 [131072, 16], P(('feat', 'dp')), may hold values from 0 to 4095, as said below
- negative_bags: int32 [8192, 16], P(('feat', 'dp')), may hold values from 0 to 4095, as said below
- relation_ids: int32 [131072], P(('feat', 'dp')), may hold values from 0 to 4095
Outputs:
- triple_loss: float32 [131072], P(('feat', 'dp'))
- new_table: bfloat16 [65536, 256], P('feat')
- new_state: float32 [65536], P('feat')
The draws below stay inside these ranges and needn't reach their ends.
Inputs may be any that keep to these rules, and one draw needn't show every extreme that they name: `slot_counts`: for every device some owner has exactly 128 live slots. `head_bags`: each entry o * 128 + c names a live slot of its device: c < slot_counts[d, o]. `tail_bags`: each entry o * 128 + c names a live slot of its device: c < slot_counts[d, o]. `negative_bags`: each entry o * 128 + c names a live slot of its device: c < slot_counts[d, o].
All inputs are finite; a program needn't handle non-finite values.
Results may differ from the reference program's by a relative error of at most 0.007.
Values may be sent and summed in bfloat16 or wider, within the bound.
No kernel may reach another device: no remote copies, remote signals or barrier semaphores. Data moves between devices by JAX's collectives and lax.ppermute only.
A program may use at most 64 MiB of HBM per device.

```python
import math
import jax
import jax.numpy as jnp
from jax import lax

D = 256
BAG = 16
RELS = 4096
ROWS_DEV = 2048
CAP = 128
NEG_DEV = 16
TRIP_DEV = 256
NEGS = 512
SLOTS = 4096
TABLE_ROWS = 65536
TRIPLES = 131072
N_FEAT = 32
N_DP = 16
DEVICES = 512


def counts_table(key):
    first, second, third = jax.random.split(jax.random.fold_in(key, 11), 3)
    level = jax.random.randint(first, (DEVICES, N_FEAT), 0, 4)
    divisor = jnp.array([1, 2, 4, 8], jnp.int32)[level]
    base = CAP // divisor
    lower = jax.random.randint(second, (DEVICES, N_FEAT), 0, 1000000) % (base // 4 + 1)
    counts = jnp.maximum(base - lower, 1)
    hottest = jax.random.randint(third, (DEVICES, 1), 0, N_FEAT)
    owners = jnp.arange(N_FEAT, dtype=jnp.int32)[None, :]
    return jnp.where(owners == hottest, CAP, counts).astype(jnp.int32)


def bag_draw(key, salt, per_device):
    counts = counts_table(key)
    first, second = jax.random.split(jax.random.fold_in(key, salt))
    total = DEVICES * per_device
    owner = jax.random.randint(first, (total, BAG), 0, N_FEAT)
    device = (jnp.arange(total, dtype=jnp.int32) // per_device)[:, None]
    limit = counts[device, owner]
    slot = jax.random.randint(second, (total, BAG), 0, limit)
    return (owner * CAP + slot).astype(jnp.int32)


def draw_slot_counts(key, part):
    return counts_table(key)


def draw_head_bags(key, part):
    return bag_draw(key, 21, TRIP_DEV)


def draw_tail_bags(key, part):
    return bag_draw(key, 22, TRIP_DEV)


def draw_negative_bags(key, part):
    return bag_draw(key, 23, NEG_DEV)


def draw_rel_diag(key, part):
    first = jax.random.fold_in(jax.random.fold_in(key, 31), 0)
    values = jnp.clip(jax.random.normal(first, (RELS, D), jnp.float32), -4.0, 4.0)
    return values.astype(jnp.bfloat16)


def place_ends(values, key, least, top_value):
    index_at = [jax.random.randint(jax.random.fold_in(key, axis), (), 0, length) for axis, length in enumerate(values.shape)]
    longest = values.shape.index(max(values.shape))
    beside = index_at[:longest] + [(index_at[longest] + 1) % values.shape[longest]] + index_at[longest + 1:]
    return values.at[tuple(index_at)].set(least).at[tuple(beside)].set(top_value)


def level_of(stream_key, extent, pieces, least, top_value):
    factor_of, own = 1.0, jax.random.fold_in(stream_key, 6)
    for position, shards_of in pieces:
        draws = jnp.exp(jax.random.uniform(jax.random.fold_in(own, position), (shards_of,), jnp.float32, least / len(pieces), top_value / len(pieces)))
        factor_of = factor_of * jnp.repeat(draws, extent[position] // shards_of).reshape([-1 if axis == position else 1 for axis in range(len(extent))])
    return factor_of


def scatter_about(stream_key, dims, scale, bound, cuts=(), held_as=jnp.bfloat16):
    result = scale * jax.random.normal(stream_key, dims, jnp.float32)
    if cuts:
        result = result * level_of(stream_key, dims, cuts, -0.22, 0.18)
    return jnp.clip(result, -bound, bound).astype(held_as)


def setup_inputs(seed: int = 0) -> dict:
    arg_keys = jax.random.split(jax.random.key(seed), 10)
    feature_table = scatter_about(arg_keys[0], (TABLE_ROWS, D), 1.0, 6.0, ((0, 32),))
    row_state = jnp.clip(jnp.exp(math.log(1.0) - 4.6051702 * jax.random.uniform(arg_keys[1], (TABLE_ROWS,), jnp.float32) ** level_of(arg_keys[1], (TABLE_ROWS,), ((0, 32),), -0.2, 0.2)), 0.01, 1.0)
    rel_diag = draw_rel_diag(jax.random.fold_in(arg_keys[9], 71), 0)
    slot_rows = place_ends(jax.random.randint(arg_keys[3], (DEVICES, N_FEAT, CAP), 0, ROWS_DEV), jax.random.fold_in(arg_keys[3], 1), 0, ROWS_DEV - 1).astype(jnp.int32)
    slot_counts = draw_slot_counts(jax.random.fold_in(arg_keys[9], 71), 0)
    head_bags = draw_head_bags(jax.random.fold_in(arg_keys[9], 71), 0)
    tail_bags = draw_tail_bags(jax.random.fold_in(arg_keys[9], 71), 0)
    negative_bags = draw_negative_bags(jax.random.fold_in(arg_keys[9], 71), 0)
    relation_ids = place_ends(jax.random.randint(arg_keys[8], (TRIPLES,), 0, RELS), jax.random.fold_in(arg_keys[8], 1), 0, RELS - 1).astype(jnp.int32)
    return dict(feature_table=feature_table, row_state=row_state, rel_diag=rel_diag, slot_rows=slot_rows, slot_counts=slot_counts, head_bags=head_bags, tail_bags=tail_bags, negative_bags=negative_bags, relation_ids=relation_ids)


score_scale = 4.0
learn_rate = 0.1

def reference(feature_table, row_state, rel_diag, slot_rows, slot_counts, head_bags, tail_bags, negative_bags, relation_ids):
    devs = N_FEAT * N_DP
    owners = jnp.arange(N_FEAT, dtype=jnp.int32) * ROWS_DEV
    global_rows = (slot_rows + owners[None, :, None]).reshape(devs, SLOTS)
    live_mask = (jnp.arange(CAP, dtype=jnp.int32)[None, None, :] < slot_counts[:, :, None]).reshape(devs, SLOTS)
    all_bags = jnp.concatenate([head_bags.reshape(devs, TRIP_DEV, BAG), tail_bags.reshape(devs, TRIP_DEV, BAG), negative_bags.reshape(devs, NEG_DEV, BAG)], axis=1)

    def pool_device(packed):
        rows_global, mask_row, bag_row = packed
        values = jnp.where(mask_row[:, None], feature_table[rows_global], jnp.zeros((), jnp.bfloat16))
        picked = values[bag_row]
        return (lax.optimization_barrier(jnp.sum(picked.astype(jnp.float32), axis=1)) / BAG).astype(jnp.bfloat16)
    entity = lax.map(pool_device, (global_rows, live_mask, all_bags))
    group_negs = entity[:, 2 * TRIP_DEV:].reshape(N_FEAT, N_DP, NEG_DEV, D).transpose(1, 0, 2, 3).reshape(N_DP, NEGS, D)
    rel_rows = relation_ids.reshape(devs, TRIP_DEV)
    groups = jnp.arange(devs, dtype=jnp.int32) % N_DP

    def score_device(carry, packed):
        ent, rel_ids, group = packed
        negs = group_negs[group]
        heads = ent[:TRIP_DEV].astype(jnp.float32)
        tails = ent[TRIP_DEV:2 * TRIP_DEV].astype(jnp.float32)
        scaling = rel_diag[rel_ids].astype(jnp.float32)
        query = (heads * scaling).astype(jnp.bfloat16)
        query_f = query.astype(jnp.float32)
        positive = score_scale * lax.optimization_barrier(jnp.sum(query_f * tails, axis=1))
        negative_score = score_scale * jnp.dot(query, negs.T, preferred_element_type=jnp.float32)
        highest = jnp.maximum(lax.optimization_barrier(jnp.max(negative_score, axis=1)), positive)
        total = jnp.exp(positive - highest) + lax.optimization_barrier(jnp.sum(jnp.exp(negative_score - highest[:, None]), axis=1))
        log_total = highest + jnp.log(total)
        loss = log_total - positive
        p_pos = jnp.exp(positive - log_total)
        p_neg = jnp.exp(negative_score - log_total[:, None]).astype(jnp.bfloat16)
        grad_query = score_scale * ((p_pos - 1.0)[:, None] * tails + jnp.dot(p_neg, negs, preferred_element_type=jnp.float32))
        grad_head = grad_query * scaling
        grad_tail = score_scale * (p_pos - 1.0)[:, None] * query_f
        part = score_scale * jnp.dot(p_neg.T, query, preferred_element_type=jnp.float32)
        return (carry.at[group].add(part), (loss, grad_head, grad_tail))
    start = jnp.zeros((N_DP, NEGS, D), jnp.float32)
    neg_sums, (losses, grad_heads, grad_tails) = lax.scan(score_device, start, (entity, rel_rows, groups))
    grad_negs = neg_sums.reshape(N_DP, N_FEAT, NEG_DEV, D).transpose(1, 0, 2, 3).reshape(devs, NEG_DEV, D)
    entity_grad = jnp.concatenate([grad_heads, grad_tails, grad_negs], axis=1) / BAG

    def spread_device(total, packed):
        rows_global, mask_row, bag_row, grads = packed
        spread = jax.ops.segment_sum(jnp.repeat(grads, BAG, axis=0), bag_row.reshape(-1), num_segments=SLOTS)
        spread = jnp.where(mask_row[:, None], spread, jnp.zeros((), jnp.float32))
        rounded = lax.optimization_barrier(spread.astype(jnp.bfloat16))
        return (total.at[rows_global].add(rounded.astype(jnp.float32)), None)
    table_grad, _ = lax.scan(spread_device, jnp.zeros((TABLE_ROWS, D), jnp.float32), (global_rows, live_mask, all_bags, entity_grad))
    new_state = row_state + lax.optimization_barrier(jnp.mean(table_grad * table_grad, axis=1))
    new_table = (feature_table.astype(jnp.float32) - learn_rate * table_grad / jnp.sqrt(new_state)[:, None]).astype(jnp.bfloat16)
    return (losses.reshape(-1), new_table, new_state)
```

```python
import jax
import jax.numpy as jnp
from jax import lax
from jax.experimental import pallas as pl
from jax.experimental.pallas import tpu as pltpu
from jax.sharding import PartitionSpec as P

score_scale = 4.0
learn_rate = 0.1
f32 = jnp.float32
bf16 = jnp.bfloat16
i32 = jnp.int32
i16 = jnp.int16

VM = pl.BlockSpec(memory_space=pltpu.VMEM)
SM = pl.BlockSpec(memory_space=pltpu.SMEM)
MIB = 1 << 20


def call(body, out_shape, in_specs, scratch=(), flops=0, moved=0, limit=48):
    outs = jax.tree.map(lambda _: VM, out_shape)
    return pl.pallas_call(
        body,
        out_shape=out_shape,
        in_specs=in_specs,
        out_specs=outs,
        scratch_shapes=list(scratch),
        compiler_params=pltpu.CompilerParams(vmem_limit_bytes=limit * MIB),
        cost_estimate=pl.CostEstimate(flops=flops, bytes_accessed=moved, transcendentals=0),
    )


def shape(dims, dtype):
    return jax.ShapeDtypeStruct(dims, dtype)


def ones_where(mask):
    return jnp.where(mask, jnp.ones((), bf16), jnp.zeros((), bf16))


def narrow_iota(dims, axis):
    return lax.broadcasted_iota(i32, dims, axis).astype(i16)


def gather_rows(asked_ref, table_ref, out_ref):
    sources, cap, width = out_ref.shape
    rows = table_ref.shape[0]
    columns = asked_ref[...].T
    lanes = narrow_iota((cap, rows), 1)
    group = 8
    for first in range(0, sources, group):
        picks = [
            ones_where(lanes == columns[:, s : s + 1].astype(i16))
            for s in range(first, first + group)
        ]
        got = jnp.dot(jnp.concatenate(picks, axis=0), table_ref[...], preferred_element_type=f32)
        out_ref[first : first + group] = got.astype(bf16).reshape(group, cap, width)


def count_entries(counts_ref, bags_ref, bags_t_ref, by_item_ref, by_slot_ref):
    items, bag = bags_ref.shape
    slots = by_slot_ref.shape[0]
    cap = slots // counts_ref.shape[1]
    lane = narrow_iota((items, cap), 1)
    sub = narrow_iota((cap, items), 0)
    lane_at = lax.broadcasted_iota(i32, (1, cap), 1)
    sub_at = lax.broadcasted_iota(i32, (cap, 1), 0)

    def step(owner, carry):
        live = counts_ref[0, owner]
        base = owner * cap
        at = pl.ds(pl.multiple_of(base, cap), cap)
        total = jnp.zeros((items, cap), bf16)
        for b in range(bag):
            entry = (bags_ref[:, b : b + 1] - base).astype(i16)
            total = total + ones_where(lane == entry)
        by_item_ref[:, at] = total * jnp.where(lane_at < live, 1.0, 0.0).astype(bf16)
        total = jnp.zeros((cap, items), bf16)
        for b in range(bag):
            entry = (bags_t_ref[b : b + 1, :] - base).astype(i16)
            total = total + ones_where(sub == entry)
        by_slot_ref[at, :] = total * jnp.where(sub_at < live, 1.0, 0.0).astype(bf16)
        return carry

    lax.fori_loop(0, counts_ref.shape[1], step, 0)


def pool_negatives(counts_ref, fetched_ref, out_ref):
    bag = 16
    trip = counts_ref.shape[0] - out_ref.shape[1]
    pooled = jnp.dot(counts_ref[trip:, :], fetched_ref[...], preferred_element_type=f32)
    entity = (pooled * (1.0 / bag)).astype(bf16)
    out_ref[...] = jnp.broadcast_to(entity[None], out_ref.shape)


def pool_triples(counts_ref, fetched_ref, scaling_ref, query_ref, tails_ref, positive_ref):
    bag = 16
    trip = query_ref.shape[0]
    pooled = jnp.dot(counts_ref[: 2 * trip, :], fetched_ref[...], preferred_element_type=f32)
    entity = (pooled * (1.0 / bag)).astype(bf16)
    tails = entity[trip:]
    query = (entity[:trip].astype(f32) * scaling_ref[...]).astype(bf16)
    query_ref[...] = query
    tails_ref[...] = tails
    positive_ref[...] = score_scale * jnp.sum(
        query.astype(f32) * tails.astype(f32), axis=1, keepdims=True
    )


def score(query_ref, tails_ref, positive_ref, scaling_ref, negs_ref, loss_ref, gneg_ref, grads_ref):
    bag = 16
    trip, width = query_ref.shape
    query = query_ref[...]
    query_f = query.astype(f32)
    tails_f = tails_ref[...].astype(f32)
    negs = negs_ref[...].reshape(-1, width)
    positive = positive_ref[...]
    scores = score_scale * lax.dot_general(
        query, negs, (((1,), (1,)), ((), ())), preferred_element_type=f32
    )
    highest = jnp.maximum(jnp.max(scores, axis=1, keepdims=True), positive)
    total = jnp.exp(positive - highest) + jnp.sum(
        jnp.exp(scores - highest), axis=1, keepdims=True
    )
    log_total = highest + jnp.log(total)
    loss_ref[...] = log_total - positive
    p_pos = jnp.exp(positive - log_total)
    p_neg_f = jnp.exp(scores - log_total)
    p_neg = p_neg_f.astype(bf16)
    gneg = score_scale * jnp.dot(p_neg_f.T.astype(bf16), query, preferred_element_type=f32)
    gneg_ref[...] = gneg.astype(bf16).reshape(gneg_ref.shape)
    grad_query = score_scale * (
        (p_pos - 1.0) * tails_f + jnp.dot(p_neg, negs, preferred_element_type=f32)
    )
    grads_ref[:trip] = (grad_query * scaling_ref[...] * (1.0 / bag)).astype(bf16)
    grads_ref[trip:] = (score_scale * (p_pos - 1.0) * query_f * (1.0 / bag)).astype(bf16)


def spread(counts_ref, grads_ref, gneg_ref, out_ref):
    bag = 16
    blocks, cap, half = out_ref.shape
    gneg = jnp.sum(gneg_ref[...].astype(f32), axis=0) * (1.0 / bag)
    grads = jnp.concatenate([grads_ref[...], gneg.astype(bf16)], axis=0)
    group = 8
    for first in range(0, blocks // 2, group):
        slot = jnp.dot(
            counts_ref[first * cap : (first + group) * cap, :], grads, preferred_element_type=f32
        ).astype(bf16)
        for s in range(group):
            for h in range(2):
                out_ref[2 * (first + s) + h] = slot[
                    s * cap : (s + 1) * cap, h * half : (h + 1) * half
                ]


def flip(p):
    return ((p & 1) << 2) | (p & 2) | (p >> 2)


def collect(place_ref, own_ref, other_ref, grads_ref, out_ref, acc_ref):
    blocks, cap, half = grads_ref.shape
    rows = acc_ref.shape[0]
    chunk = rows // 8
    place = place_ref[0]
    even = (place & 1) == 0
    asked = (
        jnp.where(even, own_ref[...], other_ref[...]),
        jnp.where(even, other_ref[...], own_ref[...]),
    )
    sub = narrow_iota((rows, cap), 0)
    group = 8
    for first in range(0, blocks, group):
        picks = [
            ones_where(sub == asked[b % 2][b // 2 : b // 2 + 1, :].astype(i16))
            for b in range(first, first + group)
        ]
        part = jnp.dot(
            jnp.concatenate(picks, axis=1),
            grads_ref[first : first + group].reshape(group * cap, half),
            preferred_element_type=f32,
        )
        acc_ref[...] = part if first == 0 else acc_ref[...] + part
    for p in range(8):
        c = flip(p) ^ (place >> 1)
        out_ref[p] = acc_ref[pl.ds(pl.multiple_of(c * chunk, chunk), chunk), :].astype(bf16)


def update(place_ref, table_ref, state_ref, own_ref, other_ref, table_out_ref, state_out_ref):
    chunk, half = own_ref.shape[1:]
    place = place_ref[0]
    even = (place & 1) == 0
    for c in range(8):
        turned = c ^ (place >> 1)
        p = flip(turned)
        own, other = own_ref[p].astype(f32), other_ref[p].astype(f32)
        gradient = jnp.concatenate(
            [jnp.where(even, own, other), jnp.where(even, other, own)], axis=1
        )
        at = slice(c * chunk, (c + 1) * chunk)
        square = jnp.sum(gradient * gradient, axis=1, keepdims=True) * (1.0 / (2 * half))
        fresh = state_ref[at, :] + square
        state_out_ref[at, :] = fresh
        table_out_ref[at, :] = (
            table_ref[at, :].astype(f32) - learn_rate * gradient / jnp.sqrt(fresh)
        ).astype(bf16)


def on_device(
    feature_table,
    row_state,
    rel_diag,
    slot_rows,
    slot_counts,
    head_bags,
    tail_bags,
    negative_bags,
    relation_ids,
):
    n_feat = lax.axis_size("feat")
    n_dp = lax.axis_size("dp")
    cap = slot_rows.shape[2]
    rows, width = feature_table.shape
    trip = head_bags.shape[0]
    n_neg = negative_bags.shape[0]
    items = 2 * trip + n_neg
    slots = n_feat * cap
    half = width // 2
    place = lax.axis_index("dp").astype(i32).reshape(1)

    def swap(value, bit):
        return lax.ppermute(value, "dp", [(i, i ^ bit) for i in range(n_dp)])

    asked = lax.all_to_all(slot_rows[0], "feat", split_axis=0, concat_axis=0, tiled=True)
    asked_other = swap(asked, 1)
    served = call(
        gather_rows,
        shape((n_feat, cap, width), bf16),
        [VM, VM],
        flops=2 * slots * rows * width,
        moved=rows * width * 2 + slots * width * 2,
    )(asked, feature_table)
    fetched = lax.all_to_all(served, "feat", split_axis=0, concat_axis=0, tiled=True)
    fetched = fetched.reshape(slots, width)

    bags = jnp.concatenate([head_bags, tail_bags, negative_bags], axis=0)
    by_item, by_slot = call(
        count_entries,
        (shape((items, slots), bf16), shape((slots, items), bf16)),
        [SM, VM, VM],
        flops=8 * items * slots * 32,
        moved=4 * items * slots,
    )(slot_counts, bags, bags.T)
    rel_pick = (
        relation_ids[:, None] == lax.broadcasted_iota(i32, (trip, rel_diag.shape[0]), 1)
    ).astype(bf16)
    scaling = jnp.dot(rel_pick, rel_diag, preferred_element_type=f32)

    own_negs = call(
        pool_negatives, shape((n_feat, n_neg, width), bf16), [VM, VM], flops=2 * n_neg * slots * width
    )(by_item, fetched)
    negs = lax.all_to_all(own_negs, "feat", split_axis=0, concat_axis=0, tiled=True)
    query, tails, positive = call(
        pool_triples,
        (shape((trip, width), bf16), shape((trip, width), bf16), shape((trip, 1), f32)),
        [VM, VM, VM],
        flops=4 * trip * slots * width,
        moved=2 * slots * width,
    )(by_item, fetched, scaling)
    loss, gneg, grads = call(
        score,
        (
            shape((trip, 1), f32),
            shape((n_feat, n_neg, width), bf16),
            shape((2 * trip, width), bf16),
        ),
        [VM] * 5,
        flops=6 * trip * n_feat * n_neg * width,
    )(query, tails, positive, scaling, negs)
    gneg = lax.all_to_all(gneg, "feat", split_axis=0, concat_axis=0, tiled=True)
    slot_grad = call(
        spread,
        shape((2 * n_feat, cap, half), bf16),
        [VM, VM, VM],
        flops=2 * items * slots * width,
    )(by_slot, grads, gneg)
    pairs = [
        [f * n_dp + 2 * p + h for f in range(n_feat) for h in range(2)] for p in range(n_dp // 2)
    ]
    arrived = lax.all_to_all(
        slot_grad,
        ("feat", "dp"),
        split_axis=0,
        concat_axis=0,
        tiled=True,
        axis_index_groups=pairs,
    )
    part = call(
        collect,
        shape((8, rows // 8, half), bf16),
        [SM, VM, VM, VM],
        scratch=[pltpu.VMEM((rows, half), f32)],
        flops=4 * slots * rows * half,
    )(place, asked, asked_other, arrived)
    kept = part
    for bit in (2, 4, 8):
        n = kept.shape[0] // 2
        kept = (kept[:n].astype(f32) + swap(kept[n:], bit).astype(f32)).astype(bf16)
    for bit in (8, 4, 2):
        kept = jnp.concatenate([kept, swap(kept, bit)], axis=0)
    across = swap(kept, 1)
    new_table, new_state = call(
        update,
        (shape((rows, width), bf16), shape((rows, 1), f32)),
        [SM, VM, VM, VM, VM],
    )(place, feature_table, row_state.reshape(rows, 1), kept, across)
    return (loss.reshape(trip), new_table, new_state.reshape(rows))


def solution(mesh):
    in_specs = (
        P("feat", None),
        P("feat"),
        P(),
        P(("feat", "dp"), None, None),
        P(("feat", "dp"), None),
        P(("feat", "dp"), None),
        P(("feat", "dp"), None),
        P(("feat", "dp"), None),
        P(("feat", "dp")),
    )
    out_specs = (P(("feat", "dp")), P("feat", None), P("feat"))
    return jax.shard_map(
        on_device, mesh=mesh, in_specs=in_specs, out_specs=out_specs, check_vma=False
    )
```

```python
import jax
import jax.numpy as jnp
from jax import lax
from jax.experimental import pallas as pl
from jax.experimental.pallas import tpu as pltpu
from jax.sharding import PartitionSpec as P

score_scale = 4.0
learn_rate = 0.1
f32 = jnp.float32
bf16 = jnp.bfloat16
i32 = jnp.int32
i16 = jnp.int16

VM = pl.BlockSpec(memory_space=pltpu.VMEM)
SM = pl.BlockSpec(memory_space=pltpu.SMEM)
MIB = 1 << 20


def call(body, out_shape, in_specs, scratch=(), flops=0, moved=0, limit=48):
    outs = jax.tree.map(lambda _: VM, out_shape)
    return pl.pallas_call(
        body,
        out_shape=out_shape,
        in_specs=in_specs,
        out_specs=outs,
        scratch_shapes=list(scratch),
        compiler_params=pltpu.CompilerParams(vmem_limit_bytes=limit * MIB),
        cost_estimate=pl.CostEstimate(flops=flops, bytes_accessed=moved, transcendentals=0),
    )


def shape(dims, dtype):
    return jax.ShapeDtypeStruct(dims, dtype)


def ones_where(mask):
    return jnp.where(mask, jnp.ones((), bf16), jnp.zeros((), bf16))


def narrow_iota(dims, axis):
    return lax.broadcasted_iota(i32, dims, axis).astype(i16)


def gather_rows(asked_ref, table_ref, out_ref):
    sources, cap, width = out_ref.shape
    rows = table_ref.shape[0]
    columns = asked_ref[...].T
    lanes = narrow_iota((cap, rows), 1)
    group = 8
    for first in range(0, sources, group):
        picks = [
            ones_where(lanes == columns[:, s : s + 1].astype(i16))
            for s in range(first, first + group)
        ]
        got = jnp.dot(jnp.concatenate(picks, axis=0), table_ref[...], preferred_element_type=f32)
        out_ref[first : first + group] = got.astype(bf16).reshape(group, cap, width)


def count_entries(counts_ref, bags_ref, by_item_ref, by_slot_ref):
    bag, items = bags_ref.shape
    owners = counts_ref.shape[1]
    cap = by_slot_ref.shape[0] // owners
    sub_at = lax.broadcasted_iota(i32, (cap, 1), 0)
    for first in range(0, items, cap):
        wide = min(cap, items - first)
        span = slice(first, first + wide)
        entries = [bags_ref[b : b + 1, span].astype(i16) for b in range(bag)]
        sub = narrow_iota((cap, wide), 0)

        def step(owner, carry):
            at = pl.ds(pl.multiple_of(owner * cap, cap), cap)
            here = sub + (owner * cap).astype(i16)
            total = ones_where(here == entries[0])
            for b in range(1, bag):
                total = total + ones_where(here == entries[b])
            total = total * jnp.where(sub_at < counts_ref[0, owner], 1.0, 0.0).astype(bf16)
            by_slot_ref[at, span] = total
            by_item_ref[span, at] = total.T
            return carry

        lax.fori_loop(0, owners, step, 0)


def pool(counts_ref, fetched_ref, scaling_ref, query_ref, tails_ref, positive_ref, negs_ref):
    bag = 16
    trip = query_ref.shape[0]
    pooled = jnp.dot(counts_ref[...], fetched_ref[...], preferred_element_type=f32)
    entity = (pooled * (1.0 / bag)).astype(bf16)
    negs_ref[...] = jnp.broadcast_to(entity[None, 2 * trip :], negs_ref.shape)
    tails = entity[trip : 2 * trip]
    query = (entity[:trip].astype(f32) * scaling_ref[...]).astype(bf16)
    query_ref[...] = query
    tails_ref[...] = tails
    positive_ref[...] = score_scale * jnp.sum(
        query.astype(f32) * tails.astype(f32), axis=1, keepdims=True
    )


def score(query_ref, tails_ref, positive_ref, scaling_ref, negs_ref, loss_ref, gneg_ref, grads_ref):
    bag = 16
    trip, width = query_ref.shape
    query = query_ref[...]
    query_f = query.astype(f32)
    tails_f = tails_ref[...].astype(f32)
    negs = negs_ref[...].reshape(-1, width)
    positive = positive_ref[...]
    scores = score_scale * lax.dot_general(
        query, negs, (((1,), (1,)), ((), ())), preferred_element_type=f32
    )
    highest = jnp.maximum(jnp.max(scores, axis=1, keepdims=True), positive)
    total = jnp.exp(positive - highest) + jnp.sum(
        jnp.exp(scores - highest), axis=1, keepdims=True
    )
    log_total = highest + jnp.log(total)
    loss_ref[...] = log_total - positive
    p_pos = jnp.exp(positive - log_total)
    p_neg_f = jnp.exp(scores - log_total)
    p_neg = p_neg_f.astype(bf16)
    gneg = score_scale * jnp.dot(p_neg_f.T.astype(bf16), query, preferred_element_type=f32)
    gneg_ref[...] = gneg.astype(bf16).reshape(gneg_ref.shape)
    grad_query = score_scale * (
        (p_pos - 1.0) * tails_f + jnp.dot(p_neg, negs, preferred_element_type=f32)
    )
    grads_ref[:trip] = (grad_query * scaling_ref[...] * (1.0 / bag)).astype(bf16)
    grads_ref[trip:] = (score_scale * (p_pos - 1.0) * query_f * (1.0 / bag)).astype(bf16)


def spread(counts_ref, grads_ref, gneg_ref, out_ref):
    bag = 16
    blocks, cap, half = out_ref.shape
    gneg = jnp.sum(gneg_ref[...].astype(f32), axis=0) * (1.0 / bag)
    grads = jnp.concatenate([grads_ref[...], gneg.astype(bf16)], axis=0)
    group = 8
    for first in range(0, blocks // 2, group):
        slot = jnp.dot(
            counts_ref[first * cap : (first + group) * cap, :], grads, preferred_element_type=f32
        ).astype(bf16)
        for s in range(group):
            for h in range(2):
                out_ref[2 * (first + s) + h] = slot[
                    s * cap : (s + 1) * cap, h * half : (h + 1) * half
                ]


def collect(place_ref, own_ref, other_ref, grads_ref, kept_ref, up_ref, down_ref, acc_ref):
    blocks, cap, half = grads_ref.shape
    rows = acc_ref.shape[0]
    chunk = rows // 8
    place = place_ref[0]
    even = (place & 1) == 0
    asked = (
        jnp.where(even, own_ref[...], other_ref[...]),
        jnp.where(even, other_ref[...], own_ref[...]),
    )
    sub = narrow_iota((rows, cap), 0)
    group = 8
    for first in range(0, blocks, group):
        picks = [
            ones_where(sub == asked[b % 2][b // 2 : b // 2 + 1, :].astype(i16))
            for b in range(first, first + group)
        ]
        part = jnp.dot(
            jnp.concatenate(picks, axis=1),
            grads_ref[first : first + group].reshape(group * cap, half),
            preferred_element_type=f32,
        )
        acc_ref[...] = part if first == 0 else acc_ref[...] + part
    parity = (place >> 1) & 1

    def take(c):
        return acc_ref[pl.ds(pl.multiple_of(c * chunk, chunk), chunk), :].astype(bf16)

    for j in range(4):
        kept_ref[j] = take(2 * j + parity)
    for j in range(2):
        up_ref[j] = take(2 * j + 1 - parity)
        down_ref[j] = take(2 * j + 5 - parity)


def update(table_ref, state_ref, sums_ref, table_out_ref, state_out_ref):
    chunk, half = sums_ref.shape[2:]
    step = state_ref.shape[1]
    eye = lax.broadcasted_iota(i32, (step, step), 0) == lax.broadcasted_iota(i32, (step, step), 1)
    for c in range(8):
        at = 2 * (c % 2)
        whole = jnp.concatenate(
            [sums_ref[at, c // 2], sums_ref[at + 1, c // 2]], axis=1
        ).astype(f32)
        for q in range(chunk // step):
            gradient = whole[q * step : (q + 1) * step]
            line = c * (chunk // step) + q
            at = slice(line * step, (line + 1) * step)
            square = jnp.sum(gradient * gradient, axis=1, keepdims=True) * (1.0 / (2 * half))
            before = jnp.sum(
                jnp.where(eye, state_ref[line : line + 1, :], 0.0), axis=1, keepdims=True
            )
            fresh = before + square
            state_out_ref[line : line + 1, :] = jnp.sum(
                jnp.where(eye, fresh, 0.0), axis=0, keepdims=True
            )
            table_out_ref[at, :] = (
                table_ref[at, :].astype(f32) - learn_rate * gradient / jnp.sqrt(fresh)
            ).astype(bf16)


def on_device(
    feature_table,
    row_state,
    rel_diag,
    slot_rows,
    slot_counts,
    head_bags,
    tail_bags,
    negative_bags,
    relation_ids,
):
    n_feat = lax.axis_size("feat")
    n_dp = lax.axis_size("dp")
    cap = slot_rows.shape[2]
    rows, width = feature_table.shape
    trip = head_bags.shape[0]
    n_neg = negative_bags.shape[0]
    items = 2 * trip + n_neg
    slots = n_feat * cap
    half = width // 2
    place = lax.axis_index("dp").astype(i32).reshape(1)

    def swap(value):
        return lax.ppermute(value, "dp", [(i, i ^ 1) for i in range(n_dp)])

    def shift(value, by):
        return lax.ppermute(value, "dp", [(i, (i + by) % n_dp) for i in range(n_dp)])

    asked = lax.all_to_all(slot_rows[0], "feat", split_axis=0, concat_axis=0, tiled=True)
    asked_other = swap(asked)
    served = call(
        gather_rows,
        shape((n_feat, cap, width), bf16),
        [VM, VM],
        flops=2 * slots * rows * width,
        moved=rows * width * 2 + slots * width * 2,
    )(asked, feature_table)
    fetched = lax.all_to_all(served, "feat", split_axis=0, concat_axis=0, tiled=True)
    fetched = fetched.reshape(slots, width)

    bags = jnp.concatenate([head_bags.T, tail_bags.T, negative_bags.T], axis=1)
    by_item, by_slot = call(
        count_entries,
        (shape((items, slots), bf16), shape((slots, items), bf16)),
        [SM, VM],
        flops=8 * items * slots * 32,
        moved=4 * items * slots,
    )(slot_counts, bags)
    rel_pick = (
        relation_ids[:, None] == lax.broadcasted_iota(i32, (trip, rel_diag.shape[0]), 1)
    ).astype(bf16)
    scaling = jnp.dot(rel_pick, rel_diag, preferred_element_type=f32)

    query, tails, positive, own_negs = call(
        pool,
        (
            shape((trip, width), bf16),
            shape((trip, width), bf16),
            shape((trip, 1), f32),
            shape((n_feat, n_neg, width), bf16),
        ),
        [VM, VM, VM],
        flops=2 * items * slots * width,
        moved=2 * slots * (width + items),
    )(by_item, fetched, scaling)
    negs = lax.all_to_all(own_negs, "feat", split_axis=0, concat_axis=0, tiled=True)
    loss, gneg, grads = call(
        score,
        (
            shape((trip, 1), f32),
            shape((n_feat, n_neg, width), bf16),
            shape((2 * trip, width), bf16),
        ),
        [VM] * 5,
        flops=6 * trip * n_feat * n_neg * width,
    )(query, tails, positive, scaling, negs)
    gneg = lax.all_to_all(gneg, "feat", split_axis=0, concat_axis=0, tiled=True)
    slot_grad = call(
        spread,
        shape((2 * n_feat, cap, half), bf16),
        [VM, VM, VM],
        flops=2 * items * slots * width,
    )(by_slot, grads, gneg)
    pairs = [
        [f * n_dp + 2 * p + h for f in range(n_feat) for h in range(2)] for p in range(n_dp // 2)
    ]
    arrived = lax.all_to_all(
        slot_grad,
        ("feat", "dp"),
        split_axis=0,
        concat_axis=0,
        tiled=True,
        axis_index_groups=pairs,
    )
    chunk = rows // 8
    kept, up, down = call(
        collect,
        (
            shape((4, chunk, half), bf16),
            shape((2, chunk, half), bf16),
            shape((2, chunk, half), bf16),
        ),
        [SM, VM, VM, VM],
        scratch=[pltpu.VMEM((rows, half), f32)],
        flops=4 * slots * rows * half,
    )(place, asked, asked_other, arrived)
    nearby = jnp.concatenate([shift(up, 2), shift(down, -2)], axis=0)
    kept = (kept.astype(f32) + nearby.astype(f32)).astype(bf16)
    apart = [[h + 4 * j for j in range(4)] for h in range(4)]
    quarter = lax.all_to_all(
        kept,
        "dp",
        split_axis=0,
        concat_axis=0,
        tiled=True,
        axis_index_groups=apart,
    )
    summed = jnp.sum(quarter.astype(f32), axis=0).astype(bf16)
    quad = lax.all_gather(summed, "dp", axis=0, axis_index_groups=apart)
    whole = lax.all_to_all(
        jnp.broadcast_to(quad[None], (4,) + quad.shape),
        "dp",
        split_axis=0,
        concat_axis=0,
        tiled=True,
        axis_index_groups=[[4 * j + h for h in range(4)] for j in range(4)],
    )
    new_table, new_state = call(
        update,
        (shape((rows, width), bf16), shape((rows // 128, 128), f32)),
        [VM] * 3,
    )(feature_table, row_state.reshape(rows // 128, 128), whole)
    return (loss.reshape(trip), new_table, new_state.reshape(rows))


def solution(mesh):
    in_specs = (
        P("feat", None),
        P("feat"),
        P(),
        P(("feat", "dp"), None, None),
        P(("feat", "dp"), None),
        P(("feat", "dp"), None),
        P(("feat", "dp"), None),
        P(("feat", "dp"), None),
        P(("feat", "dp")),
    )
    out_specs = (P(("feat", "dp")), P("feat", None), P("feat"))
    return jax.shard_map(
        on_device, mesh=mesh, in_specs=in_specs, out_specs=out_specs, check_vma=False
    )
```

```python
import jax
import jax.numpy as jnp
from jax import lax
from jax.experimental import pallas as pl
from jax.experimental.pallas import tpu as pltpu
from jax.sharding import PartitionSpec as P

score_scale = 4.0
learn_rate = 0.1
f32 = jnp.float32
bf16 = jnp.bfloat16
i32 = jnp.int32
i16 = jnp.int16

VM = pl.BlockSpec(memory_space=pltpu.VMEM)
SM = pl.BlockSpec(memory_space=pltpu.SMEM)
MIB = 1 << 20
LIMIT = 60


def call(
    body, out_shape, in_specs, out_specs=None, grid=(), scratch=(), flops=0, moved=0
):
    if out_specs is None:
        out_specs = jax.tree.map(lambda _: VM, out_shape)
    return pl.pallas_call(
        body,
        out_shape=out_shape,
        grid=grid,
        in_specs=in_specs,
        out_specs=out_specs,
        scratch_shapes=list(scratch),
        compiler_params=pltpu.CompilerParams(vmem_limit_bytes=LIMIT * MIB),
        cost_estimate=pl.CostEstimate(flops=flops, bytes_accessed=moved, transcendentals=0),
    )


def cut(dims, axis):
    return pl.BlockSpec(dims, lambda step: tuple(step if d == axis else 0 for d in range(len(dims))))


def whole(dims):
    return pl.BlockSpec(dims, lambda step: (0,) * len(dims))


def shape(dims, dtype):
    return jax.ShapeDtypeStruct(dims, dtype)


def ones_where(mask):
    return jnp.where(mask, jnp.ones((), bf16), jnp.zeros((), bf16))


def narrow_iota(dims, axis):
    return lax.broadcasted_iota(i32, dims, axis).astype(i16)


def gather_rows(asked_ref, table_ref, out_ref):
    sources, cap, width = out_ref.shape
    columns = asked_ref[...].T
    lanes = narrow_iota((cap, table_ref.shape[0]), 1)
    picks = [ones_where(lanes == columns[:, s : s + 1].astype(i16)) for s in range(sources)]
    got = jnp.dot(jnp.concatenate(picks, axis=0), table_ref[...], preferred_element_type=f32)
    out_ref[...] = got.astype(bf16).reshape(sources, cap, width)


def count_entries(counts_ref, bags_ref, by_item_ref, by_slot_ref):
    bag, items = bags_ref.shape
    owners = counts_ref.shape[1]
    cap = by_slot_ref.shape[0] // owners
    sub_at = lax.broadcasted_iota(i32, (cap, 1), 0)
    for first in range(0, items, cap):
        wide = min(cap, items - first)
        span = slice(first, first + wide)
        entries = [bags_ref[b : b + 1, span].astype(i16) for b in range(bag)]
        sub = narrow_iota((cap, wide), 0)

        def step(owner, carry):
            at = pl.ds(pl.multiple_of(owner * cap, cap), cap)
            here = sub + (owner * cap).astype(i16)
            total = ones_where(here == entries[0])
            for b in range(1, bag):
                total = total + ones_where(here == entries[b])
            total = total * jnp.where(sub_at < counts_ref[0, owner], 1.0, 0.0).astype(bf16)
            by_slot_ref[at, span] = total
            by_item_ref[span, at] = total.T
            return carry

        lax.fori_loop(0, owners, step, 0)


def pool(
    counts_ref, fetched_ref, scaling_ref, query_ref, tails_ref, positive_ref, negs_ref, pooled_ref
):
    bag = 16
    trip = query_ref.shape[0]
    part = jnp.dot(counts_ref[...], fetched_ref[...], preferred_element_type=f32)

    @pl.when(pl.program_id(0) == 0)
    def _():
        pooled_ref[...] = part

    @pl.when(pl.program_id(0) > 0)
    def _():
        pooled_ref[...] += part

    @pl.when(pl.program_id(0) == pl.num_programs(0) - 1)
    def _():
        entity = (pooled_ref[...] * (1.0 / bag)).astype(bf16)
        negs_ref[...] = jnp.broadcast_to(entity[None, 2 * trip :], negs_ref.shape)
        tails = entity[trip : 2 * trip]
        query = (entity[:trip].astype(f32) * scaling_ref[...]).astype(bf16)
        query_ref[...] = query
        tails_ref[...] = tails
        positive_ref[...] = score_scale * jnp.sum(
            query.astype(f32) * tails.astype(f32), axis=1, keepdims=True
        )


def score(query_ref, tails_ref, positive_ref, scaling_ref, negs_ref, loss_ref, gneg_ref, grads_ref):
    bag = 16
    trip, width = query_ref.shape
    query = query_ref[...]
    query_f = query.astype(f32)
    tails_f = tails_ref[...].astype(f32)
    negs = negs_ref[...].reshape(-1, width)
    positive = positive_ref[...]
    scores = score_scale * lax.dot_general(
        query, negs, (((1,), (1,)), ((), ())), preferred_element_type=f32
    )
    highest = jnp.maximum(jnp.max(scores, axis=1, keepdims=True), positive)
    total = jnp.exp(positive - highest) + jnp.sum(
        jnp.exp(scores - highest), axis=1, keepdims=True
    )
    log_total = highest + jnp.log(total)
    loss_ref[...] = log_total - positive
    p_pos = jnp.exp(positive - log_total)
    p_neg_f = jnp.exp(scores - log_total)
    p_neg = p_neg_f.astype(bf16)
    gneg = score_scale * jnp.dot(p_neg_f.T.astype(bf16), query, preferred_element_type=f32)
    gneg_ref[...] = gneg.astype(bf16).reshape(gneg_ref.shape)
    grad_query = score_scale * (
        (p_pos - 1.0) * tails_f + jnp.dot(p_neg, negs, preferred_element_type=f32)
    )
    grads_ref[:trip] = (grad_query * scaling_ref[...] * (1.0 / bag)).astype(bf16)
    grads_ref[trip:] = (score_scale * (p_pos - 1.0) * query_f * (1.0 / bag)).astype(bf16)


def spread(counts_ref, grads_ref, gneg_ref, out_ref, all_ref):
    bag = 16
    trips = grads_ref.shape[0]

    @pl.when(pl.program_id(0) == 0)
    def _():
        gneg = jnp.sum(gneg_ref[...].astype(f32), axis=0) * (1.0 / bag)
        all_ref[:trips] = grads_ref[...]
        all_ref[trips:] = gneg.astype(bf16)

    slot = jnp.dot(counts_ref[...], all_ref[...], preferred_element_type=f32)
    out_ref[...] = slot.astype(bf16).reshape(out_ref.shape)


def collect(asked_ref, grads_ref, out_ref, acc_ref):
    sources, cap, width = grads_ref.shape
    sub = narrow_iota((acc_ref.shape[0], cap), 0)
    picks = [ones_where(sub == asked_ref[s : s + 1, :].astype(i16)) for s in range(sources)]
    part = jnp.dot(
        jnp.concatenate(picks, axis=1),
        grads_ref[...].reshape(sources * cap, width),
        preferred_element_type=f32,
    )
    step, last = pl.program_id(0), pl.num_programs(0) - 1

    @pl.when(step == 0)
    def _():
        acc_ref[...] = part

    @pl.when((step > 0) & (step < last))
    def _():
        acc_ref[...] += part

    @pl.when(step == last)
    def _():
        out_ref[...] = (acc_ref[...] + part).astype(bf16)


def update(table_ref, state_ref, sums_ref, table_out_ref, state_out_ref):
    lines, step = state_ref.shape
    width = table_ref.shape[1]
    eye = lax.broadcasted_iota(i32, (step, step), 0) == lax.broadcasted_iota(i32, (step, step), 1)
    for line in range(lines):
        at = slice(line * step, (line + 1) * step)
        gradient = sums_ref[at, :].astype(f32)
        square = jnp.sum(gradient * gradient, axis=1, keepdims=True) * (1.0 / width)
        before = jnp.sum(
            jnp.where(eye, state_ref[line : line + 1, :], 0.0), axis=1, keepdims=True
        )
        fresh = before + square
        state_out_ref[line : line + 1, :] = jnp.sum(
            jnp.where(eye, fresh, 0.0), axis=0, keepdims=True
        )
        table_out_ref[at, :] = (
            table_ref[at, :].astype(f32) - learn_rate * gradient / jnp.sqrt(fresh)
        ).astype(bf16)


def on_device(
    feature_table,
    row_state,
    rel_diag,
    slot_rows,
    slot_counts,
    head_bags,
    tail_bags,
    negative_bags,
    relation_ids,
):
    n_feat = lax.axis_size("feat")
    n_dp = lax.axis_size("dp")
    cap = slot_rows.shape[2]
    rows, width = feature_table.shape
    trip = head_bags.shape[0]
    n_neg = negative_bags.shape[0]
    items = 2 * trip + n_neg
    slots = n_feat * cap
    steps = 4
    part = n_feat // steps
    asked = lax.all_to_all(slot_rows[0], "feat", split_axis=0, concat_axis=0, tiled=True)
    served = call(
        gather_rows,
        shape((n_feat, cap, width), bf16),
        [cut((part, cap), 0), whole((rows, width))],
        cut((part, cap, width), 0),
        grid=(steps,),
        flops=2 * slots * rows * width,
        moved=rows * width * 2 + slots * width * 2,
    )(asked, feature_table)
    fetched = lax.all_to_all(served, "feat", split_axis=0, concat_axis=0, tiled=True)
    fetched = fetched.reshape(slots, width)

    bags = jnp.concatenate([head_bags.T, tail_bags.T, negative_bags.T], axis=1)
    by_item, by_slot = call(
        count_entries,
        (shape((items, slots), bf16), shape((slots, items), bf16)),
        [SM, VM],
        flops=8 * items * slots * 32,
        moved=4 * items * slots,
    )(slot_counts, bags)
    rel_pick = (
        relation_ids[:, None] == lax.broadcasted_iota(i32, (trip, rel_diag.shape[0]), 1)
    ).astype(bf16)
    scaling = jnp.dot(rel_pick, rel_diag, preferred_element_type=f32)

    query, tails, positive, own_negs = call(
        pool,
        (
            shape((trip, width), bf16),
            shape((trip, width), bf16),
            shape((trip, 1), f32),
            shape((n_feat, n_neg, width), bf16),
        ),
        [cut((items, slots // steps), 1), cut((slots // steps, width), 0), whole((trip, width))],
        (whole((trip, width)), whole((trip, width)), whole((trip, 1)), whole((n_feat, n_neg, width))),
        grid=(steps,),
        scratch=[pltpu.VMEM((items, width), f32)],
        flops=2 * items * slots * width,
        moved=2 * slots * (width + items),
    )(by_item, fetched, scaling)
    negs = lax.all_to_all(own_negs, "feat", split_axis=0, concat_axis=0, tiled=True)
    loss, gneg, grads = call(
        score,
        (
            shape((trip, 1), f32),
            shape((n_feat, n_neg, width), bf16),
            shape((2 * trip, width), bf16),
        ),
        [VM] * 5,
        flops=6 * trip * n_feat * n_neg * width,
    )(query, tails, positive, scaling, negs)
    gneg = lax.all_to_all(gneg, "feat", split_axis=0, concat_axis=0, tiled=True)
    slot_grad = call(
        spread,
        shape((n_feat, cap, width), bf16),
        [
            cut((slots // steps, items), 0),
            whole((2 * trip, width)),
            whole((n_feat, n_neg, width)),
        ],
        cut((part, cap, width), 0),
        grid=(steps,),
        scratch=[pltpu.VMEM((items, width), bf16)],
        flops=2 * items * slots * width,
        moved=2 * slots * (width + items),
    )(by_slot, grads, gneg)
    arrived = lax.all_to_all(slot_grad, "feat", split_axis=0, concat_axis=0, tiled=True)
    sums = call(
        collect,
        shape((rows, width), bf16),
        [cut((part, cap), 0), cut((part, cap, width), 0)],
        whole((rows, width)),
        grid=(steps,),
        scratch=[pltpu.VMEM((rows, width), f32)],
        flops=2 * slots * rows * width,
        moved=2 * (slots + rows) * width,
    )(asked, arrived)
    close = [[4 * j + h for h in range(4)] for j in range(n_dp // 4)]
    apart = [[h + 4 * j for j in range(n_dp // 4)] for h in range(4)]

    def exchange(value, groups):
        return lax.all_to_all(
            value, "dp", split_axis=0, concat_axis=0, tiled=True, axis_index_groups=groups
        )

    for groups in (close, apart):
        pieces = exchange(sums.reshape(4, -1, width), groups)
        sums = jnp.sum(pieces.astype(f32), axis=0).astype(bf16)
    quad = lax.all_gather(sums, "dp", axis=0, axis_index_groups=apart)
    sums = exchange(jnp.broadcast_to(quad[None], (4,) + quad.shape), close).reshape(rows, width)
    lines = rows // cap
    new_table, new_state = call(
        update,
        (shape((rows, width), bf16), shape((lines, cap), f32)),
        [cut((rows // 2, width), 0), cut((lines // 2, cap), 0), cut((rows // 2, width), 0)],
        (cut((rows // 2, width), 0), cut((lines // 2, cap), 0)),
        grid=(2,),
        flops=8 * rows * width,
        moved=6 * rows * width,
    )(feature_table, row_state.reshape(lines, cap), sums)
    return (loss.reshape(trip), new_table, new_state.reshape(rows))


def solution(mesh):
    in_specs = (
        P("feat", None),
        P("feat"),
        P(),
        P(("feat", "dp"), None, None),
        P(("feat", "dp"), None),
        P(("feat", "dp"), None),
        P(("feat", "dp"), None),
        P(("feat", "dp"), None),
        P(("feat", "dp")),
    )
    out_specs = (P(("feat", "dp")), P("feat", None), P("feat"))
    return jax.shard_map(
        on_device, mesh=mesh, in_specs=in_specs, out_specs=out_specs, check_vma=False
    )
```

```python
import jax
import jax.numpy as jnp
from jax import lax
from jax.experimental import pallas as pl
from jax.experimental.pallas import tpu as pltpu
from jax.sharding import PartitionSpec as P

score_scale = 4.0
learn_rate = 0.1
f32 = jnp.float32
bf16 = jnp.bfloat16
i32 = jnp.int32
i16 = jnp.int16

VM = pl.BlockSpec(memory_space=pltpu.VMEM)
SM = pl.BlockSpec(memory_space=pltpu.SMEM)
MIB = 1 << 20
LIMIT = 48


def call(body, out_shape, in_specs, scratch=(), flops=0, moved=0, limit=LIMIT):
    outs = jax.tree.map(lambda _: VM, out_shape)
    return pl.pallas_call(
        body,
        out_shape=out_shape,
        in_specs=in_specs,
        out_specs=outs,
        scratch_shapes=list(scratch),
        compiler_params=pltpu.CompilerParams(vmem_limit_bytes=limit * MIB),
        cost_estimate=pl.CostEstimate(flops=flops, bytes_accessed=moved, transcendentals=0),
    )


def shape(dims, dtype):
    return jax.ShapeDtypeStruct(dims, dtype)


def ones_where(mask):
    return jnp.where(mask, jnp.ones((), bf16), jnp.zeros((), bf16))


def narrow_iota(dims, axis):
    return lax.broadcasted_iota(i32, dims, axis).astype(i16)


def gather_rows(place_ref, asked_ref, table_ref, out_ref):
    sources, cap, width = out_ref.shape
    rows = table_ref.shape[0]
    even = (place_ref[0] & 1) == 0
    columns = asked_ref[...].T
    lanes = narrow_iota((cap, rows), 1)
    group = 8
    for first in range(0, sources, group):
        picks = []
        for s in range(first, first + group):
            column = jnp.where(
                even, columns[:, 2 * s : 2 * s + 1], columns[:, 2 * s + 1 : 2 * s + 2]
            )
            picks.append(ones_where(lanes == column.astype(i16)))
        got = jnp.dot(jnp.concatenate(picks, axis=0), table_ref[...], preferred_element_type=f32)
        out_ref[first : first + group] = got.astype(bf16).reshape(group, cap, width)


def count_entries(counts_ref, bags_ref, neg_ref, by_item_ref, by_slot_ref):
    bag, trips = bags_ref.shape
    negs = neg_ref.shape[0]
    owners = counts_ref.shape[1]
    cap = by_slot_ref.shape[0] // owners
    sub_at = lax.broadcasted_iota(i32, (cap, 1), 0)
    lane_at = lax.broadcasted_iota(i32, (1, cap), 1)
    sub = narrow_iota((cap, cap), 0)
    for first in range(0, trips, cap):
        span = slice(first, first + cap)
        entries = [bags_ref[b : b + 1, span].astype(i16) for b in range(bag)]

        def step(pair, carry):
            for owner in (2 * pair, 2 * pair + 1):
                at = pl.ds(pl.multiple_of(owner * cap, cap), cap)
                here = sub + (owner * cap).astype(i16)
                total = ones_where(here == entries[0])
                for b in range(1, bag):
                    total = total + ones_where(here == entries[b])
                total = total * jnp.where(sub_at < counts_ref[0, owner], 1.0, 0.0).astype(bf16)
                by_slot_ref[at, span] = total
                by_item_ref[span, at] = total.T
            return carry

        lax.fori_loop(0, owners // 2, step, 0)

    lane = narrow_iota((negs, cap), 1)
    columns = [
        jnp.broadcast_to(neg_ref[:, b : b + 1], (negs, cap)).astype(i16) for b in range(bag)
    ]
    span = slice(trips, trips + negs)

    def last(owner, carry):
        at = pl.ds(pl.multiple_of(owner * cap, cap), cap)
        here = lane + (owner * cap).astype(i16)
        total = ones_where(here == columns[0])
        for b in range(1, bag):
            total = total + ones_where(here == columns[b])
        total = total * jnp.where(lane_at < counts_ref[0, owner], 1.0, 0.0).astype(bf16)
        by_item_ref[span, at] = total
        by_slot_ref[at, span] = total.T
        return carry

    lax.fori_loop(0, owners, last, 0)


def pick_relations(ids_ref, rel_ref, out_ref):
    step = ids_ref.shape[1]
    relations = rel_ref.shape[0]
    eye = lax.broadcasted_iota(i32, (step, step), 0) == lax.broadcasted_iota(i32, (step, step), 1)
    lanes = narrow_iota((step, relations), 1)
    for line in range(ids_ref.shape[0]):
        column = jnp.sum(jnp.where(eye, ids_ref[line : line + 1, :], 0), axis=1, keepdims=True)
        pick = ones_where(lanes == column.astype(i16))
        out_ref[line * step : (line + 1) * step, :] = jnp.dot(
            pick, rel_ref[...], preferred_element_type=f32
        )


def pool(counts_ref, fetched_ref, scaling_ref, query_ref, tails_ref, positive_ref, negs_ref):
    bag = 16
    trip = query_ref.shape[0]
    pooled = jnp.dot(counts_ref[...], fetched_ref[...], preferred_element_type=f32)
    entity = (pooled * (1.0 / bag)).astype(bf16)
    negs_ref[...] = jnp.broadcast_to(entity[None, 2 * trip :], negs_ref.shape)
    tails = entity[trip : 2 * trip]
    query = (entity[:trip].astype(f32) * scaling_ref[...]).astype(bf16)
    query_ref[...] = query
    tails_ref[...] = tails
    positive_ref[...] = score_scale * jnp.sum(
        query.astype(f32) * tails.astype(f32), axis=1, keepdims=True
    )


def score(query_ref, tails_ref, positive_ref, scaling_ref, negs_ref, loss_ref, gneg_ref, grads_ref):
    bag = 16
    trip, width = query_ref.shape
    query = query_ref[...]
    query_f = query.astype(f32)
    tails_f = tails_ref[...].astype(f32)
    negs = negs_ref[...].reshape(-1, width)
    positive = positive_ref[...]
    scores = score_scale * lax.dot_general(
        query, negs, (((1,), (1,)), ((), ())), preferred_element_type=f32
    )
    highest = jnp.maximum(jnp.max(scores, axis=1, keepdims=True), positive)
    total = jnp.exp(positive - highest) + jnp.sum(
        jnp.exp(scores - highest), axis=1, keepdims=True
    )
    log_total = highest + jnp.log(total)
    loss = log_total - positive
    step = loss_ref.shape[1]
    eye = lax.broadcasted_iota(i32, (step, step), 0) == lax.broadcasted_iota(i32, (step, step), 1)
    for line in range(loss_ref.shape[0]):
        part = loss[line * step : (line + 1) * step]
        loss_ref[line : line + 1, :] = jnp.sum(jnp.where(eye, part, 0.0), axis=0, keepdims=True)
    p_pos = jnp.exp(positive - log_total)
    p_neg_f = jnp.exp(scores - log_total)
    p_neg = p_neg_f.astype(bf16)
    gneg = score_scale * jnp.dot(p_neg_f.T.astype(bf16), query, preferred_element_type=f32)
    gneg_ref[...] = gneg.astype(bf16).reshape(gneg_ref.shape)
    grad_query = score_scale * (
        (p_pos - 1.0) * tails_f + jnp.dot(p_neg, negs, preferred_element_type=f32)
    )
    grads_ref[:trip] = (grad_query * scaling_ref[...] * (1.0 / bag)).astype(bf16)
    grads_ref[trip:] = (score_scale * (p_pos - 1.0) * query_f * (1.0 / bag)).astype(bf16)


def spread(counts_ref, grads_ref, gneg_ref, out_ref):
    bag = 16
    blocks, cap, half = out_ref.shape
    gneg = jnp.sum(gneg_ref[...].astype(f32), axis=0) * (1.0 / bag)
    grads = jnp.concatenate([grads_ref[...], gneg.astype(bf16)], axis=0)
    group = 8
    for first in range(0, blocks // 2, group):
        slot = jnp.dot(
            counts_ref[first * cap : (first + group) * cap, :], grads, preferred_element_type=f32
        ).astype(bf16)
        for s in range(group):
            for h in range(2):
                out_ref[2 * (first + s) + h] = slot[
                    s * cap : (s + 1) * cap, h * half : (h + 1) * half
                ]


def collect(place_ref, asked_ref, grads_ref, kept_ref, up_ref, down_ref, acc_ref):
    blocks, cap, half = grads_ref.shape
    rows = acc_ref.shape[0]
    chunk = rows // 8
    place = place_ref[0]
    sub = narrow_iota((rows, cap), 0)
    group = 8
    for first in range(0, blocks, group):
        picks = [
            ones_where(sub == asked_ref[b : b + 1, :].astype(i16))
            for b in range(first, first + group)
        ]
        part = jnp.dot(
            jnp.concatenate(picks, axis=1),
            grads_ref[first : first + group].reshape(group * cap, half),
            preferred_element_type=f32,
        )
        acc_ref[...] = part if first == 0 else acc_ref[...] + part
    parity = (place >> 1) & 1

    def take(c):
        return acc_ref[pl.ds(pl.multiple_of(c * chunk, chunk), chunk), :].astype(bf16)

    for j in range(4):
        kept_ref[j] = take(2 * j + parity)
    for j in range(2):
        up_ref[j] = take(2 * j + 1 - parity)
        down_ref[j] = take(2 * j + 5 - parity)


def update(table_ref, state_ref, sums_ref, table_out_ref, state_out_ref):
    chunk, half = sums_ref.shape[2:]
    step = state_ref.shape[1]
    eye = lax.broadcasted_iota(i32, (step, step), 0) == lax.broadcasted_iota(i32, (step, step), 1)
    for c in range(8):
        at = 2 * (c % 2)
        whole = jnp.concatenate(
            [sums_ref[at, c // 2], sums_ref[at + 1, c // 2]], axis=1
        ).astype(f32)
        for q in range(chunk // step):
            gradient = whole[q * step : (q + 1) * step]
            line = c * (chunk // step) + q
            at = slice(line * step, (line + 1) * step)
            square = jnp.sum(gradient * gradient, axis=1, keepdims=True) * (1.0 / (2 * half))
            before = jnp.sum(
                jnp.where(eye, state_ref[line : line + 1, :], 0.0), axis=1, keepdims=True
            )
            fresh = before + square
            state_out_ref[line : line + 1, :] = jnp.sum(
                jnp.where(eye, fresh, 0.0), axis=0, keepdims=True
            )
            table_out_ref[at, :] = (
                table_ref[at, :].astype(f32) - learn_rate * gradient / jnp.sqrt(fresh)
            ).astype(bf16)


def on_device(
    feature_table,
    row_state,
    rel_diag,
    slot_rows,
    slot_counts,
    head_bags,
    tail_bags,
    negative_bags,
    relation_ids,
):
    n_feat = lax.axis_size("feat")
    n_dp = lax.axis_size("dp")
    cap = slot_rows.shape[2]
    rows, width = feature_table.shape
    trip = head_bags.shape[0]
    n_neg = negative_bags.shape[0]
    items = 2 * trip + n_neg
    slots = n_feat * cap
    half = width // 2
    place = lax.axis_index("dp").astype(i32).reshape(1)

    def shift(value, by):
        return lax.ppermute(value, "dp", [(i, (i + by) % n_dp) for i in range(n_dp)])

    pairs = [
        [f * n_dp + 2 * p + h for f in range(n_feat) for h in range(2)] for p in range(n_dp // 2)
    ]

    def across_pairs(value):
        return lax.all_to_all(
            value,
            ("feat", "dp"),
            split_axis=0,
            concat_axis=0,
            tiled=True,
            axis_index_groups=pairs,
        )

    place, slot_rows = lax.optimization_barrier((place, slot_rows))
    twice = jnp.broadcast_to(slot_rows[0][:, None], (n_feat, 2, cap)).reshape(2 * n_feat, cap)
    asked = across_pairs(twice)
    served = call(
        gather_rows,
        shape((n_feat, cap, width), bf16),
        [SM, VM, VM],
        flops=2 * slots * rows * width,
        moved=rows * width * 2 + slots * width * 2,
    )(place, asked, feature_table)
    fetched = lax.all_to_all(served, "feat", split_axis=0, concat_axis=0, tiled=True)
    fetched = fetched.reshape(slots, width)

    bags = jnp.concatenate([head_bags.T, tail_bags.T], axis=1)
    by_item, by_slot = call(
        count_entries,
        (shape((items, slots), bf16), shape((slots, items), bf16)),
        [SM, VM, VM],
        flops=8 * items * slots * 32,
        moved=4 * items * slots,
    )(slot_counts, bags, negative_bags)
    scaling = call(
        pick_relations,
        shape((trip, width), f32),
        [VM, VM],
        flops=2 * trip * rel_diag.shape[0] * width,
        moved=2 * rel_diag.shape[0] * width,
    )(relation_ids.reshape(trip // cap, cap), rel_diag)

    query, tails, positive, own_negs = call(
        pool,
        (
            shape((trip, width), bf16),
            shape((trip, width), bf16),
            shape((trip, 1), f32),
            shape((n_feat, n_neg, width), bf16),
        ),
        [VM, VM, VM],
        flops=2 * items * slots * width,
        moved=2 * slots * (width + items),
    )(by_item, fetched, scaling)
    negs = lax.all_to_all(own_negs, "feat", split_axis=0, concat_axis=0, tiled=True)
    loss, gneg, grads = call(
        score,
        (
            shape((trip // cap, cap), f32),
            shape((n_feat, n_neg, width), bf16),
            shape((2 * trip, width), bf16),
        ),
        [VM] * 5,
        flops=6 * trip * n_feat * n_neg * width,
    )(query, tails, positive, scaling, negs)
    gneg = lax.all_to_all(gneg, "feat", split_axis=0, concat_axis=0, tiled=True)
    slot_grad = call(
        spread,
        shape((2 * n_feat, cap, half), bf16),
        [VM, VM, VM],
        flops=2 * items * slots * width,
    )(by_slot, grads, gneg)
    arrived = across_pairs(slot_grad)
    chunk = rows // 8
    kept, up, down = call(
        collect,
        (
            shape((4, chunk, half), bf16),
            shape((2, chunk, half), bf16),
            shape((2, chunk, half), bf16),
        ),
        [SM, VM, VM],
        scratch=[pltpu.VMEM((rows, half), f32)],
        flops=4 * slots * rows * half,
    )(place, asked, arrived)
    nearby = jnp.concatenate([shift(up, 2), shift(down, -2)], axis=0)
    kept = (kept.astype(f32) + nearby.astype(f32)).astype(bf16)
    apart = [[h + 4 * j for j in range(4)] for h in range(4)]
    quarter = lax.all_to_all(
        kept,
        "dp",
        split_axis=0,
        concat_axis=0,
        tiled=True,
        axis_index_groups=apart,
    )
    summed = jnp.sum(quarter.astype(f32), axis=0).astype(bf16)
    quad = lax.all_gather(summed, "dp", axis=0, axis_index_groups=apart)
    whole = lax.all_to_all(
        jnp.broadcast_to(quad[None], (4,) + quad.shape),
        "dp",
        split_axis=0,
        concat_axis=0,
        tiled=True,
        axis_index_groups=[[4 * j + h for h in range(4)] for j in range(4)],
    )
    new_table, new_state = call(
        update,
        (shape((rows, width), bf16), shape((rows // 128, 128), f32)),
        [VM] * 3,
    )(feature_table, row_state.reshape(rows // 128, 128), whole)
    return (loss.reshape(trip), new_table, new_state.reshape(rows))


def solution(mesh):
    in_specs = (
        P("feat", None),
        P("feat"),
        P(),
        P(("feat", "dp"), None, None),
        P(("feat", "dp"), None),
        P(("feat", "dp"), None),
        P(("feat", "dp"), None),
        P(("feat", "dp"), None),
        P(("feat", "dp")),
    )
    out_specs = (P(("feat", "dp")), P("feat", None), P("feat"))
    return jax.shard_map(
        on_device, mesh=mesh, in_specs=in_specs, out_specs=out_specs, check_vma=False
    )
```

```python
import jax
import jax.numpy as jnp
from jax import lax
from jax.experimental import pallas as pl
from jax.experimental.pallas import tpu as pltpu
from jax.sharding import PartitionSpec as P

score_scale = 4.0
learn_rate = 0.1
f32 = jnp.float32
bf16 = jnp.bfloat16
i32 = jnp.int32
i16 = jnp.int16

VM = pl.BlockSpec(memory_space=pltpu.VMEM)
SM = pl.BlockSpec(memory_space=pltpu.SMEM)
MIB = 1 << 20
LIMIT = 48


def call(body, out_shape, in_specs, scratch=(), flops=0, moved=0, limit=LIMIT):
    outs = jax.tree.map(lambda _: VM, out_shape)
    return pl.pallas_call(
        body,
        out_shape=out_shape,
        in_specs=in_specs,
        out_specs=outs,
        scratch_shapes=list(scratch),
        compiler_params=pltpu.CompilerParams(vmem_limit_bytes=limit * MIB),
        cost_estimate=pl.CostEstimate(flops=flops, bytes_accessed=moved, transcendentals=0),
    )


def shape(dims, dtype):
    return jax.ShapeDtypeStruct(dims, dtype)


def ones_where(mask):
    return jnp.where(mask, jnp.ones((), bf16), jnp.zeros((), bf16))


def narrow_iota(dims, axis):
    return lax.broadcasted_iota(i32, dims, axis).astype(i16)


def gather_rows(place_ref, asked_ref, table_ref, out_ref):
    sources, cap, width = out_ref.shape
    rows = table_ref.shape[0]
    even = (place_ref[0] & 1) == 0
    columns = asked_ref[...].T
    lanes = narrow_iota((cap, rows), 1)
    group = 8
    for first in range(0, sources, group):
        picks = []
        for s in range(first, first + group):
            column = jnp.where(
                even, columns[:, 2 * s : 2 * s + 1], columns[:, 2 * s + 1 : 2 * s + 2]
            )
            picks.append(ones_where(lanes == column.astype(i16)))
        got = jnp.dot(jnp.concatenate(picks, axis=0), table_ref[...], preferred_element_type=f32)
        out_ref[first : first + group] = got.astype(bf16).reshape(group, cap, width)


def count_entries(counts_ref, bags_ref, neg_ref, by_item_ref, by_slot_ref):
    bag, trips = bags_ref.shape
    negs = neg_ref.shape[0]
    owners = counts_ref.shape[1]
    cap = by_slot_ref.shape[0] // owners
    sub_at = lax.broadcasted_iota(i32, (cap, 1), 0)
    lane_at = lax.broadcasted_iota(i32, (1, cap), 1)
    sub = narrow_iota((cap, cap), 0)
    for first in range(0, trips, cap):
        span = slice(first, first + cap)
        entries = [bags_ref[b : b + 1, span].astype(i16) for b in range(bag)]

        def step(pair, carry):
            for owner in (2 * pair, 2 * pair + 1):
                at = pl.ds(pl.multiple_of(owner * cap, cap), cap)
                here = sub + (owner * cap).astype(i16)
                total = ones_where(here == entries[0])
                for b in range(1, bag):
                    total = total + ones_where(here == entries[b])
                total = total * jnp.where(sub_at < counts_ref[0, owner], 1.0, 0.0).astype(bf16)
                by_slot_ref[at, span] = total
                by_item_ref[span, at] = total.T
            return carry

        lax.fori_loop(0, owners // 2, step, 0)

    lane = narrow_iota((negs, cap), 1)
    columns = [
        jnp.broadcast_to(neg_ref[:, b : b + 1], (negs, cap)).astype(i16) for b in range(bag)
    ]
    span = slice(trips, trips + negs)

    def last(owner, carry):
        at = pl.ds(pl.multiple_of(owner * cap, cap), cap)
        here = lane + (owner * cap).astype(i16)
        total = ones_where(here == columns[0])
        for b in range(1, bag):
            total = total + ones_where(here == columns[b])
        total = total * jnp.where(lane_at < counts_ref[0, owner], 1.0, 0.0).astype(bf16)
        by_item_ref[span, at] = total
        by_slot_ref[at, span] = total.T
        return carry

    lax.fori_loop(0, owners, last, 0)


def pick_relations(ids_ref, rel_ref, out_ref):
    step = ids_ref.shape[1]
    relations = rel_ref.shape[0]
    eye = lax.broadcasted_iota(i32, (step, step), 0) == lax.broadcasted_iota(i32, (step, step), 1)
    lanes = narrow_iota((step, relations), 1)
    for line in range(ids_ref.shape[0]):
        column = jnp.sum(jnp.where(eye, ids_ref[line : line + 1, :], 0), axis=1, keepdims=True)
        pick = ones_where(lanes == column.astype(i16))
        out_ref[line * step : (line + 1) * step, :] = jnp.dot(
            pick, rel_ref[...], preferred_element_type=f32
        )


def pool(counts_ref, fetched_ref, scaling_ref, query_ref, tails_ref, positive_ref, negs_ref):
    bag = 16
    trip = query_ref.shape[0]
    pooled = jnp.dot(counts_ref[...], fetched_ref[...], preferred_element_type=f32)
    entity = (pooled * (1.0 / bag)).astype(bf16)
    negs_ref[...] = jnp.broadcast_to(entity[None, 2 * trip :], negs_ref.shape)
    tails = entity[trip : 2 * trip]
    query = (entity[:trip].astype(f32) * scaling_ref[...]).astype(bf16)
    query_ref[...] = query
    tails_ref[...] = tails
    positive_ref[...] = score_scale * jnp.sum(
        query.astype(f32) * tails.astype(f32), axis=1, keepdims=True
    )


def score(query_ref, tails_ref, positive_ref, scaling_ref, negs_ref, loss_ref, gneg_ref, grads_ref):
    bag = 16
    trip, width = query_ref.shape
    query = query_ref[...]
    query_f = query.astype(f32)
    tails_f = tails_ref[...].astype(f32)
    negs = negs_ref[...].reshape(-1, width)
    positive = positive_ref[...]
    scores = score_scale * lax.dot_general(
        query, negs, (((1,), (1,)), ((), ())), preferred_element_type=f32
    )
    highest = jnp.maximum(jnp.max(scores, axis=1, keepdims=True), positive)
    total = jnp.exp(positive - highest) + jnp.sum(
        jnp.exp(scores - highest), axis=1, keepdims=True
    )
    log_total = highest + jnp.log(total)
    loss = log_total - positive
    step = loss_ref.shape[1]
    eye = lax.broadcasted_iota(i32, (step, step), 0) == lax.broadcasted_iota(i32, (step, step), 1)
    for line in range(loss_ref.shape[0]):
        part = loss[line * step : (line + 1) * step]
        loss_ref[line : line + 1, :] = jnp.sum(jnp.where(eye, part, 0.0), axis=0, keepdims=True)
    p_pos = jnp.exp(positive - log_total)
    p_neg_f = jnp.exp(scores - log_total)
    p_neg = p_neg_f.astype(bf16)
    gneg = score_scale * jnp.dot(p_neg_f.T.astype(bf16), query, preferred_element_type=f32)
    gneg_ref[...] = gneg.astype(bf16).reshape(gneg_ref.shape)
    grad_query = score_scale * (
        (p_pos - 1.0) * tails_f + jnp.dot(p_neg, negs, preferred_element_type=f32)
    )
    grads_ref[:trip] = (grad_query * scaling_ref[...] * (1.0 / bag)).astype(bf16)
    grads_ref[trip:] = (score_scale * (p_pos - 1.0) * query_f * (1.0 / bag)).astype(bf16)


def spread(counts_ref, grads_ref, gneg_ref, out_ref):
    bag = 16
    blocks, cap, half = out_ref.shape
    gneg = jnp.sum(gneg_ref[...].astype(f32), axis=0) * (1.0 / bag)
    grads = jnp.concatenate([grads_ref[...], gneg.astype(bf16)], axis=0)
    group = 8
    for first in range(0, blocks // 2, group):
        slot = jnp.dot(
            counts_ref[first * cap : (first + group) * cap, :], grads, preferred_element_type=f32
        ).astype(bf16)
        for s in range(group):
            for h in range(2):
                out_ref[2 * (first + s) + h] = slot[
                    s * cap : (s + 1) * cap, h * half : (h + 1) * half
                ]


def collect(place_ref, asked_ref, grads_ref, kept_ref, up_ref, down_ref, acc_ref):
    blocks, cap, half = grads_ref.shape
    rows = acc_ref.shape[0]
    chunk = rows // 8
    place = place_ref[0]
    sub = narrow_iota((rows, cap), 0)
    group = 8
    for first in range(0, blocks, group):
        picks = [
            ones_where(sub == asked_ref[b : b + 1, :].astype(i16))
            for b in range(first, first + group)
        ]
        part = jnp.dot(
            jnp.concatenate(picks, axis=1),
            grads_ref[first : first + group].reshape(group * cap, half),
            preferred_element_type=f32,
        )
        acc_ref[...] = part if first == 0 else acc_ref[...] + part
    parity = (place >> 1) & 1

    def take(c):
        return acc_ref[pl.ds(pl.multiple_of(c * chunk, chunk), chunk), :].astype(bf16)

    for j in range(4):
        kept_ref[j] = take(2 * j + parity)
    for j in range(2):
        up_ref[j] = take(2 * j + 1 - parity)
        down_ref[j] = take(2 * j + 5 - parity)


def update(
    place_ref,
    table_ref,
    state_ref,
    own_ref,
    below_ref,
    above_ref,
    low_ref,
    high_ref,
    table_out_ref,
    state_out_ref,
    sums_ref,
):
    half = own_ref.shape[2]
    chunk = own_ref.shape[1]
    kind = place_ref[0] & 3
    sums_ref[kind] = own_ref[...]
    sums_ref[(kind + 3) & 3] = below_ref[...]
    sums_ref[(kind + 1) & 3] = above_ref[...]
    sums_ref[(kind + 2) & 3, :2] = low_ref[...]
    sums_ref[(kind + 2) & 3, 2:] = high_ref[...]
    step = state_ref.shape[1]
    eye = lax.broadcasted_iota(i32, (step, step), 0) == lax.broadcasted_iota(i32, (step, step), 1)
    for c in range(8):
        at = 2 * (c % 2)
        whole = jnp.concatenate(
            [sums_ref[at, c // 2], sums_ref[at + 1, c // 2]], axis=1
        ).astype(f32)
        for q in range(chunk // step):
            gradient = whole[q * step : (q + 1) * step]
            line = c * (chunk // step) + q
            at = slice(line * step, (line + 1) * step)
            square = jnp.sum(gradient * gradient, axis=1, keepdims=True) * (1.0 / (2 * half))
            before = jnp.sum(
                jnp.where(eye, state_ref[line : line + 1, :], 0.0), axis=1, keepdims=True
            )
            fresh = before + square
            state_out_ref[line : line + 1, :] = jnp.sum(
                jnp.where(eye, fresh, 0.0), axis=0, keepdims=True
            )
            table_out_ref[at, :] = (
                table_ref[at, :].astype(f32) - learn_rate * gradient / jnp.sqrt(fresh)
            ).astype(bf16)


def on_device(
    feature_table,
    row_state,
    rel_diag,
    slot_rows,
    slot_counts,
    head_bags,
    tail_bags,
    negative_bags,
    relation_ids,
):
    n_feat = lax.axis_size("feat")
    n_dp = lax.axis_size("dp")
    cap = slot_rows.shape[2]
    rows, width = feature_table.shape
    trip = head_bags.shape[0]
    n_neg = negative_bags.shape[0]
    items = 2 * trip + n_neg
    slots = n_feat * cap
    half = width // 2
    place = lax.axis_index("dp").astype(i32).reshape(1)

    def shift(value, by):
        return lax.ppermute(value, "dp", [(i, (i + by) % n_dp) for i in range(n_dp)])

    pairs = [
        [f * n_dp + 2 * p + h for f in range(n_feat) for h in range(2)] for p in range(n_dp // 2)
    ]

    def across_pairs(value):
        return lax.all_to_all(
            value,
            ("feat", "dp"),
            split_axis=0,
            concat_axis=0,
            tiled=True,
            axis_index_groups=pairs,
        )

    place, slot_rows = lax.optimization_barrier((place, slot_rows))
    twice = jnp.broadcast_to(slot_rows[0][:, None], (n_feat, 2, cap)).reshape(2 * n_feat, cap)
    asked = across_pairs(twice)
    served = call(
        gather_rows,
        shape((n_feat, cap, width), bf16),
        [SM, VM, VM],
        flops=2 * slots * rows * width,
        moved=rows * width * 2 + slots * width * 2,
    )(place, asked, feature_table)
    fetched = lax.all_to_all(served, "feat", split_axis=0, concat_axis=0, tiled=True)
    fetched = fetched.reshape(slots, width)

    bags = jnp.concatenate([head_bags.T, tail_bags.T], axis=1)
    by_item, by_slot = call(
        count_entries,
        (shape((items, slots), bf16), shape((slots, items), bf16)),
        [SM, VM, VM],
        flops=8 * items * slots * 32,
        moved=4 * items * slots,
    )(slot_counts, bags, negative_bags)
    scaling = call(
        pick_relations,
        shape((trip, width), f32),
        [VM, VM],
        flops=2 * trip * rel_diag.shape[0] * width,
        moved=2 * rel_diag.shape[0] * width,
    )(relation_ids.reshape(trip // cap, cap), rel_diag)

    query, tails, positive, own_negs = call(
        pool,
        (
            shape((trip, width), bf16),
            shape((trip, width), bf16),
            shape((trip, 1), f32),
            shape((n_feat, n_neg, width), bf16),
        ),
        [VM, VM, VM],
        flops=2 * items * slots * width,
        moved=2 * slots * (width + items),
    )(by_item, fetched, scaling)
    negs = lax.all_to_all(own_negs, "feat", split_axis=0, concat_axis=0, tiled=True)
    loss, gneg, grads = call(
        score,
        (
            shape((trip // cap, cap), f32),
            shape((n_feat, n_neg, width), bf16),
            shape((2 * trip, width), bf16),
        ),
        [VM] * 5,
        limit=24,
        flops=6 * trip * n_feat * n_neg * width,
    )(query, tails, positive, scaling, negs)
    gneg = lax.all_to_all(gneg, "feat", split_axis=0, concat_axis=0, tiled=True)
    slot_grad = call(
        spread,
        shape((2 * n_feat, cap, half), bf16),
        [VM, VM, VM],
        limit=24,
        flops=2 * items * slots * width,
    )(by_slot, grads, gneg)
    arrived = across_pairs(slot_grad)
    chunk = rows // 8
    kept, up, down = call(
        collect,
        (
            shape((4, chunk, half), bf16),
            shape((2, chunk, half), bf16),
            shape((2, chunk, half), bf16),
        ),
        [SM, VM, VM],
        scratch=[pltpu.VMEM((rows, half), f32)],
        flops=4 * slots * rows * half,
    )(place, asked, arrived)
    nearby = jnp.concatenate([shift(up, 2), shift(down, -2)], axis=0)
    kept = (kept.astype(f32) + nearby.astype(f32)).astype(bf16)
    apart = [[h + 4 * j for j in range(4)] for h in range(4)]
    quarter = lax.all_to_all(
        kept,
        "dp",
        split_axis=0,
        concat_axis=0,
        tiled=True,
        axis_index_groups=apart,
    )
    summed = jnp.sum(quarter.astype(f32), axis=0).astype(bf16)
    quad = lax.all_gather(summed, "dp", axis=0, axis_index_groups=apart)
    below, above = shift(quad, 1), shift(quad, -1)
    low, high = shift(quad[:2], 2), shift(quad[2:], -2)
    new_table, new_state = call(
        update,
        (shape((rows, width), bf16), shape((rows // 128, 128), f32)),
        [SM] + [VM] * 7,
        scratch=[pltpu.VMEM((4, 4, chunk, half), bf16)],
    )(place, feature_table, row_state.reshape(rows // 128, 128), quad, below, above, low, high)
    return (loss.reshape(trip), new_table, new_state.reshape(rows))


def solution(mesh):
    in_specs = (
        P("feat", None),
        P("feat"),
        P(),
        P(("feat", "dp"), None, None),
        P(("feat", "dp"), None),
        P(("feat", "dp"), None),
        P(("feat", "dp"), None),
        P(("feat", "dp"), None),
        P(("feat", "dp")),
    )
    out_specs = (P(("feat", "dp")), P("feat", None), P("feat"))
    return jax.shard_map(
        on_device, mesh=mesh, in_specs=in_specs, out_specs=out_specs, check_vma=False
    )
```

```python
import functools

import jax
import jax.numpy as jnp
from jax import lax
from jax.experimental import pallas as pl
from jax.experimental.pallas import tpu as pltpu
from jax.sharding import PartitionSpec as P

score_scale = 4.0
learn_rate = 0.1
f32 = jnp.float32
bf16 = jnp.bfloat16
i32 = jnp.int32
i16 = jnp.int16

VM = pl.BlockSpec(memory_space=pltpu.VMEM)
SM = pl.BlockSpec(memory_space=pltpu.SMEM)
MIB = 1 << 20
LIMIT = 48


def call(body, out_shape, in_specs, scratch=(), flops=0, moved=0, limit=LIMIT):
    outs = jax.tree.map(lambda _: VM, out_shape)
    return pl.pallas_call(
        body,
        out_shape=out_shape,
        in_specs=in_specs,
        out_specs=outs,
        scratch_shapes=list(scratch),
        compiler_params=pltpu.CompilerParams(vmem_limit_bytes=limit * MIB),
        cost_estimate=pl.CostEstimate(flops=flops, bytes_accessed=moved, transcendentals=0),
    )


def shape(dims, dtype):
    return jax.ShapeDtypeStruct(dims, dtype)


def ones_where(mask):
    return jnp.where(mask, jnp.ones((), bf16), jnp.zeros((), bf16))


def narrow_iota(dims, axis):
    return lax.broadcasted_iota(i32, dims, axis).astype(i16)


def gather_rows(place_ref, asked_ref, table_ref, out_ref):
    sources, cap, width = out_ref.shape
    rows = table_ref.shape[0]
    even = (place_ref[0] & 1) == 0
    columns = asked_ref[...].T
    lanes = narrow_iota((cap, rows), 1)
    group = 8
    for first in range(0, sources, group):
        picks = []
        for s in range(first, first + group):
            column = jnp.where(
                even, columns[:, 2 * s : 2 * s + 1], columns[:, 2 * s + 1 : 2 * s + 2]
            )
            picks.append(ones_where(lanes == column.astype(i16)))
        got = jnp.dot(jnp.concatenate(picks, axis=0), table_ref[...], preferred_element_type=f32)
        out_ref[first : first + group] = got.astype(bf16).reshape(group, cap, width)


def count_entries(counts_ref, bags_ref, neg_ref, by_item_ref, by_slot_ref):
    bag, trips = bags_ref.shape
    negs = neg_ref.shape[0]
    owners = counts_ref.shape[1]
    cap = by_slot_ref.shape[0] // owners
    sub_at = lax.broadcasted_iota(i32, (cap, 1), 0)
    lane_at = lax.broadcasted_iota(i32, (1, cap), 1)
    sub = narrow_iota((cap, cap), 0)
    for first in range(0, trips, cap):
        span = slice(first, first + cap)
        entries = [bags_ref[b : b + 1, span].astype(i16) for b in range(bag)]

        def step(pair, carry):
            for owner in (2 * pair, 2 * pair + 1):
                at = pl.ds(pl.multiple_of(owner * cap, cap), cap)
                here = sub + (owner * cap).astype(i16)
                total = ones_where(here == entries[0])
                for b in range(1, bag):
                    total = total + ones_where(here == entries[b])
                total = total * jnp.where(sub_at < counts_ref[0, owner], 1.0, 0.0).astype(bf16)
                by_slot_ref[at, span] = total
                by_item_ref[span, at] = total.T
            return carry

        lax.fori_loop(0, owners // 2, step, 0)

    lane = narrow_iota((negs, cap), 1)
    columns = [
        jnp.broadcast_to(neg_ref[:, b : b + 1], (negs, cap)).astype(i16) for b in range(bag)
    ]
    span = slice(trips, trips + negs)

    def last(owner, carry):
        at = pl.ds(pl.multiple_of(owner * cap, cap), cap)
        here = lane + (owner * cap).astype(i16)
        total = ones_where(here == columns[0])
        for b in range(1, bag):
            total = total + ones_where(here == columns[b])
        total = total * jnp.where(lane_at < counts_ref[0, owner], 1.0, 0.0).astype(bf16)
        by_item_ref[span, at] = total
        by_slot_ref[at, span] = total.T
        return carry

    lax.fori_loop(0, owners, last, 0)


def pick_relations(ids_ref, rel_ref, out_ref):
    step = ids_ref.shape[1]
    relations = rel_ref.shape[0]
    eye = lax.broadcasted_iota(i32, (step, step), 0) == lax.broadcasted_iota(i32, (step, step), 1)
    lanes = narrow_iota((step, relations), 1)
    for line in range(ids_ref.shape[0]):
        column = jnp.sum(jnp.where(eye, ids_ref[line : line + 1, :], 0), axis=1, keepdims=True)
        pick = ones_where(lanes == column.astype(i16))
        out_ref[line * step : (line + 1) * step, :] = jnp.dot(
            pick, rel_ref[...], preferred_element_type=f32
        )


def pool(counts_ref, fetched_ref, scaling_ref, query_ref, tails_ref, positive_ref, negs_ref):
    bag = 16
    trip = query_ref.shape[0]
    pooled = jnp.dot(counts_ref[...], fetched_ref[...], preferred_element_type=f32)
    entity = (pooled * (1.0 / bag)).astype(bf16)
    negs_ref[...] = jnp.broadcast_to(entity[None, 2 * trip :], negs_ref.shape)
    tails = entity[trip : 2 * trip]
    query = (entity[:trip].astype(f32) * scaling_ref[...]).astype(bf16)
    query_ref[...] = query
    tails_ref[...] = tails
    positive_ref[...] = score_scale * jnp.sum(
        query.astype(f32) * tails.astype(f32), axis=1, keepdims=True
    )


def score(query_ref, tails_ref, positive_ref, scaling_ref, negs_ref, loss_ref, gneg_ref, grads_ref):
    bag = 16
    trip, width = query_ref.shape
    query = query_ref[...]
    query_f = query.astype(f32)
    tails_f = tails_ref[...].astype(f32)
    negs = negs_ref[...].reshape(-1, width)
    positive = positive_ref[...]
    scores = score_scale * lax.dot_general(
        query, negs, (((1,), (1,)), ((), ())), preferred_element_type=f32
    )
    highest = jnp.maximum(jnp.max(scores, axis=1, keepdims=True), positive)
    total = jnp.exp(positive - highest) + jnp.sum(
        jnp.exp(scores - highest), axis=1, keepdims=True
    )
    log_total = highest + jnp.log(total)
    loss = log_total - positive
    step = loss_ref.shape[1]
    eye = lax.broadcasted_iota(i32, (step, step), 0) == lax.broadcasted_iota(i32, (step, step), 1)
    for line in range(loss_ref.shape[0]):
        part = loss[line * step : (line + 1) * step]
        loss_ref[line : line + 1, :] = jnp.sum(jnp.where(eye, part, 0.0), axis=0, keepdims=True)
    p_pos = jnp.exp(positive - log_total)
    p_neg_f = jnp.exp(scores - log_total)
    p_neg = p_neg_f.astype(bf16)
    gneg = score_scale * jnp.dot(p_neg_f.T.astype(bf16), query, preferred_element_type=f32)
    gneg_ref[...] = gneg.astype(bf16).reshape(gneg_ref.shape)
    grad_query = score_scale * (
        (p_pos - 1.0) * tails_f + jnp.dot(p_neg, negs, preferred_element_type=f32)
    )
    grads_ref[:trip] = (grad_query * scaling_ref[...] * (1.0 / bag)).astype(bf16)
    grads_ref[trip:] = (score_scale * (p_pos - 1.0) * query_f * (1.0 / bag)).astype(bf16)


def spread(counts_ref, grads_ref, gneg_ref, out_ref):
    bag = 16
    blocks, cap, half = out_ref.shape
    gneg = jnp.sum(gneg_ref[...].astype(f32), axis=0) * (1.0 / bag)
    grads = jnp.concatenate([grads_ref[...], gneg.astype(bf16)], axis=0)
    group = 8
    for first in range(0, blocks // 2, group):
        slot = jnp.dot(
            counts_ref[first * cap : (first + group) * cap, :], grads, preferred_element_type=f32
        ).astype(bf16)
        for s in range(group):
            for h in range(2):
                out_ref[2 * (first + s) + h] = slot[
                    s * cap : (s + 1) * cap, h * half : (h + 1) * half
                ]


def collect(turn, place_ref, asked_ref, grads_ref, *refs):
    out_refs, acc_ref = refs[:-1], refs[-1]
    blocks, cap, half = grads_ref.shape
    chunk = acc_ref.shape[1] // 4
    parity = (place_ref[0] >> 1) & 1
    parity = 1 - parity if turn else parity
    lane = lax.broadcasted_iota(i32, (cap, 4 * chunk), 1)
    row = (lane + (lane // chunk + parity) * chunk).astype(i16)
    columns = asked_ref[...].T
    group = 8
    for first in range(0, blocks, group):
        picks = [
            ones_where(row == columns[:, b : b + 1].astype(i16))
            for b in range(first, first + group)
        ]
        part = jnp.dot(
            grads_ref[first : first + group].reshape(group * cap, half).T,
            jnp.concatenate(picks, axis=0),
            preferred_element_type=f32,
        )
        acc_ref[...] = part if first == 0 else acc_ref[...] + part
    j = 0
    for ref in out_refs:
        for k in range(ref.shape[0]):
            ref[k] = acc_ref[:, j * chunk : (j + 1) * chunk].T.astype(bf16)
            j += 1


def update(
    place_ref,
    table_ref,
    state_ref,
    own_ref,
    below_ref,
    above_ref,
    low_ref,
    high_ref,
    table_out_ref,
    state_out_ref,
    sums_ref,
):
    half = own_ref.shape[2]
    chunk = own_ref.shape[1]
    kind = place_ref[0] & 3
    sums_ref[kind] = own_ref[...]
    sums_ref[(kind + 3) & 3] = below_ref[...]
    sums_ref[(kind + 1) & 3] = above_ref[...]
    sums_ref[(kind + 2) & 3, :2] = low_ref[...]
    sums_ref[(kind + 2) & 3, 2:] = high_ref[...]
    step = state_ref.shape[1]
    eye = lax.broadcasted_iota(i32, (step, step), 0) == lax.broadcasted_iota(i32, (step, step), 1)
    for c in range(8):
        at = 2 * (c % 2)
        whole = jnp.concatenate(
            [sums_ref[at, c // 2], sums_ref[at + 1, c // 2]], axis=1
        ).astype(f32)
        for q in range(chunk // step):
            gradient = whole[q * step : (q + 1) * step]
            line = c * (chunk // step) + q
            at = slice(line * step, (line + 1) * step)
            square = jnp.sum(gradient * gradient, axis=1, keepdims=True) * (1.0 / (2 * half))
            before = jnp.sum(
                jnp.where(eye, state_ref[line : line + 1, :], 0.0), axis=1, keepdims=True
            )
            fresh = before + square
            state_out_ref[line : line + 1, :] = jnp.sum(
                jnp.where(eye, fresh, 0.0), axis=0, keepdims=True
            )
            table_out_ref[at, :] = (
                table_ref[at, :].astype(f32) - learn_rate * gradient / jnp.sqrt(fresh)
            ).astype(bf16)


def on_device(
    feature_table,
    row_state,
    rel_diag,
    slot_rows,
    slot_counts,
    head_bags,
    tail_bags,
    negative_bags,
    relation_ids,
):
    n_feat = lax.axis_size("feat")
    n_dp = lax.axis_size("dp")
    cap = slot_rows.shape[2]
    rows, width = feature_table.shape
    trip = head_bags.shape[0]
    n_neg = negative_bags.shape[0]
    items = 2 * trip + n_neg
    slots = n_feat * cap
    half = width // 2
    place = lax.axis_index("dp").astype(i32).reshape(1)

    def shift(value, by):
        return lax.ppermute(value, "dp", [(i, (i + by) % n_dp) for i in range(n_dp)])

    pairs = [
        [f * n_dp + 2 * p + h for f in range(n_feat) for h in range(2)] for p in range(n_dp // 2)
    ]

    def across_pairs(value):
        return lax.all_to_all(
            value,
            ("feat", "dp"),
            split_axis=0,
            concat_axis=0,
            tiled=True,
            axis_index_groups=pairs,
        )

    place, slot_rows = lax.optimization_barrier((place, slot_rows))
    twice = jnp.broadcast_to(slot_rows[0][:, None], (n_feat, 2, cap)).reshape(2 * n_feat, cap)
    asked = across_pairs(twice)
    served = call(
        gather_rows,
        shape((n_feat, cap, width), bf16),
        [SM, VM, VM],
        flops=2 * slots * rows * width,
        moved=rows * width * 2 + slots * width * 2,
    )(place, asked, feature_table)
    fetched = lax.all_to_all(served, "feat", split_axis=0, concat_axis=0, tiled=True)
    fetched = fetched.reshape(slots, width)

    bags = jnp.concatenate([head_bags.T, tail_bags.T], axis=1)
    by_item, by_slot = call(
        count_entries,
        (shape((items, slots), bf16), shape((slots, items), bf16)),
        [SM, VM, VM],
        flops=8 * items * slots * 32,
        moved=4 * items * slots,
    )(slot_counts, bags, negative_bags)
    scaling = call(
        pick_relations,
        shape((trip, width), f32),
        [VM, VM],
        flops=2 * trip * rel_diag.shape[0] * width,
        moved=2 * rel_diag.shape[0] * width,
    )(relation_ids.reshape(trip // cap, cap), rel_diag)

    query, tails, positive, own_negs = call(
        pool,
        (
            shape((trip, width), bf16),
            shape((trip, width), bf16),
            shape((trip, 1), f32),
            shape((n_feat, n_neg, width), bf16),
        ),
        [VM, VM, VM],
        flops=2 * items * slots * width,
        moved=2 * slots * (width + items),
    )(by_item, fetched, scaling)
    negs = lax.all_to_all(own_negs, "feat", split_axis=0, concat_axis=0, tiled=True)
    loss, gneg, grads = call(
        score,
        (
            shape((trip // cap, cap), f32),
            shape((n_feat, n_neg, width), bf16),
            shape((2 * trip, width), bf16),
        ),
        [VM] * 5,
        limit=24,
        flops=6 * trip * n_feat * n_neg * width,
    )(query, tails, positive, scaling, negs)
    gneg = lax.all_to_all(gneg, "feat", split_axis=0, concat_axis=0, tiled=True)
    slot_grad = call(
        spread,
        shape((2 * n_feat, cap, half), bf16),
        [VM, VM, VM],
        limit=24,
        flops=2 * items * slots * width,
    )(by_slot, grads, gneg)
    arrived = across_pairs(slot_grad)
    chunk = rows // 8
    scratch = [pltpu.VMEM((half, 4 * chunk), f32)]
    up, down = call(
        functools.partial(collect, 1),
        (shape((2, chunk, half), bf16), shape((2, chunk, half), bf16)),
        [SM, VM, VM],
        scratch=scratch,
        flops=2 * slots * rows * half,
    )(place, asked, arrived)
    kept = call(
        functools.partial(collect, 0),
        shape((4, chunk, half), bf16),
        [SM, VM, VM],
        scratch=scratch,
        flops=2 * slots * rows * half,
        moved=2 * slots * width,
    )(place, asked, arrived)
    nearby = jnp.concatenate([shift(up, 2), shift(down, -2)], axis=0)
    kept = (kept.astype(f32) + nearby.astype(f32)).astype(bf16)
    apart = [[h + 4 * j for j in range(4)] for h in range(4)]
    quarter = lax.all_to_all(
        kept,
        "dp",
        split_axis=0,
        concat_axis=0,
        tiled=True,
        axis_index_groups=apart,
    )
    summed = jnp.sum(quarter.astype(f32), axis=0).astype(bf16)
    quad = lax.all_gather(summed, "dp", axis=0, axis_index_groups=apart)
    below, above = shift(quad, 1), shift(quad, -1)
    low, high = shift(quad[:2], 2), shift(quad[2:], -2)
    new_table, new_state = call(
        update,
        (shape((rows, width), bf16), shape((rows // 128, 128), f32)),
        [SM] + [VM] * 7,
        scratch=[pltpu.VMEM((4, 4, chunk, half), bf16)],
    )(place, feature_table, row_state.reshape(rows // 128, 128), quad, below, above, low, high)
    return (loss.reshape(trip), new_table, new_state.reshape(rows))


def solution(mesh):
    in_specs = (
        P("feat", None),
        P("feat"),
        P(),
        P(("feat", "dp"), None, None),
        P(("feat", "dp"), None),
        P(("feat", "dp"), None),
        P(("feat", "dp"), None),
        P(("feat", "dp"), None),
        P(("feat", "dp")),
    )
    out_specs = (P(("feat", "dp")), P("feat", None), P("feat"))
    return jax.shard_map(
        on_device, mesh=mesh, in_specs=in_specs, out_specs=out_specs, check_vma=False
    )
```

```python
import functools

import jax
import jax.numpy as jnp
from jax import lax
from jax.experimental import pallas as pl
from jax.experimental.pallas import tpu as pltpu
from jax.sharding import PartitionSpec as P

score_scale = 4.0
learn_rate = 0.1
f32 = jnp.float32
bf16 = jnp.bfloat16
i32 = jnp.int32
i16 = jnp.int16

VM = pl.BlockSpec(memory_space=pltpu.VMEM)
SM = pl.BlockSpec(memory_space=pltpu.SMEM)
MIB = 1 << 20
LIMIT = 48


def call(body, out_shape, in_specs, scratch=(), flops=0, moved=0, limit=LIMIT):
    outs = jax.tree.map(lambda _: VM, out_shape)
    return pl.pallas_call(
        body,
        out_shape=out_shape,
        in_specs=in_specs,
        out_specs=outs,
        scratch_shapes=list(scratch),
        compiler_params=pltpu.CompilerParams(vmem_limit_bytes=limit * MIB),
        cost_estimate=pl.CostEstimate(flops=flops, bytes_accessed=moved, transcendentals=0),
    )


def shape(dims, dtype):
    return jax.ShapeDtypeStruct(dims, dtype)


def ones_where(mask):
    return jnp.where(mask, jnp.ones((), bf16), jnp.zeros((), bf16))


def narrow_iota(dims, axis):
    return lax.broadcasted_iota(i32, dims, axis).astype(i16)


def gather_rows(place_ref, asked_ref, table_ref, out_ref):
    sources, cap, width = out_ref.shape
    rows = table_ref.shape[0]
    even = (place_ref[0] & 1) == 0
    columns = asked_ref[...].T
    lanes = narrow_iota((cap, rows), 1)
    group = 8
    for first in range(0, sources, group):
        picks = []
        for s in range(first, first + group):
            column = jnp.where(
                even, columns[:, 2 * s : 2 * s + 1], columns[:, 2 * s + 1 : 2 * s + 2]
            )
            picks.append(ones_where(lanes == column.astype(i16)))
        got = jnp.dot(jnp.concatenate(picks, axis=0), table_ref[...], preferred_element_type=f32)
        out_ref[first : first + group] = got.astype(bf16).reshape(group, cap, width)


def count_entries(counts_ref, bags_ref, neg_ref, by_item_ref, by_slot_ref):
    bag, trips = bags_ref.shape
    negs = neg_ref.shape[0]
    owners = counts_ref.shape[1]
    cap = by_slot_ref.shape[0] // owners
    sub_at = lax.broadcasted_iota(i32, (cap, 1), 0)
    lane_at = lax.broadcasted_iota(i32, (1, cap), 1)
    sub = narrow_iota((cap, cap), 0)
    for first in range(0, trips, cap):
        span = slice(first, first + cap)
        entries = [bags_ref[b : b + 1, span].astype(i16) for b in range(bag)]

        def step(pair, carry):
            for owner in (2 * pair, 2 * pair + 1):
                at = pl.ds(pl.multiple_of(owner * cap, cap), cap)
                here = sub + (owner * cap).astype(i16)
                total = ones_where(here == entries[0])
                for b in range(1, bag):
                    total = total + ones_where(here == entries[b])
                total = total * jnp.where(sub_at < counts_ref[0, owner], 1.0, 0.0).astype(bf16)
                by_slot_ref[at, span] = total
                by_item_ref[span, at] = total.T
            return carry

        lax.fori_loop(0, owners // 2, step, 0)

    lane = narrow_iota((negs, cap), 1)
    columns = [
        jnp.broadcast_to(neg_ref[:, b : b + 1], (negs, cap)).astype(i16) for b in range(bag)
    ]
    span = slice(trips, trips + negs)

    def last(owner, carry):
        at = pl.ds(pl.multiple_of(owner * cap, cap), cap)
        here = lane + (owner * cap).astype(i16)
        total = ones_where(here == columns[0])
        for b in range(1, bag):
            total = total + ones_where(here == columns[b])
        total = total * jnp.where(lane_at < counts_ref[0, owner], 1.0, 0.0).astype(bf16)
        by_item_ref[span, at] = total
        by_slot_ref[at, span] = total.T
        return carry

    lax.fori_loop(0, owners, last, 0)


def pick_relations(ids_ref, rel_ref, out_ref):
    step = ids_ref.shape[1]
    relations = rel_ref.shape[0]
    eye = lax.broadcasted_iota(i32, (step, step), 0) == lax.broadcasted_iota(i32, (step, step), 1)
    lanes = narrow_iota((step, relations), 1)
    for line in range(ids_ref.shape[0]):
        column = jnp.sum(jnp.where(eye, ids_ref[line : line + 1, :], 0), axis=1, keepdims=True)
        pick = ones_where(lanes == column.astype(i16))
        out_ref[line * step : (line + 1) * step, :] = jnp.dot(
            pick, rel_ref[...], preferred_element_type=f32
        )


def pool(
    counts_ref,
    fetched_ref,
    scaling_ref,
    query_ref,
    tails_ref,
    positive_ref,
    negs_ref,
    held_ref,
    sems,
):
    bag = 16
    trip = query_ref.shape[0]
    pieces = sems.shape[0]
    wide = fetched_ref.shape[0] // pieces
    spans = [slice(k * wide, (k + 1) * wide) for k in range(pieces)]
    copies = [
        pltpu.make_async_copy(counts_ref.at[:, span], held_ref.at[:, span], sems.at[k])
        for k, span in enumerate(spans)
    ]
    for copy in copies:
        copy.start()
    pooled = None
    for copy, span in zip(copies, spans):
        copy.wait()
        part = jnp.dot(held_ref[:, span], fetched_ref[span, :], preferred_element_type=f32)
        pooled = part if pooled is None else pooled + part
    entity = (pooled * (1.0 / bag)).astype(bf16)
    negs_ref[...] = jnp.broadcast_to(entity[None, 2 * trip :], negs_ref.shape)
    tails = entity[trip : 2 * trip]
    query = (entity[:trip].astype(f32) * scaling_ref[...]).astype(bf16)
    query_ref[...] = query
    tails_ref[...] = tails
    positive_ref[...] = score_scale * jnp.sum(
        query.astype(f32) * tails.astype(f32), axis=1, keepdims=True
    )


def score(query_ref, tails_ref, positive_ref, scaling_ref, negs_ref, loss_ref, gneg_ref, grads_ref):
    bag = 16
    trip, width = query_ref.shape
    query = query_ref[...]
    query_f = query.astype(f32)
    tails_f = tails_ref[...].astype(f32)
    negs = negs_ref[...].reshape(-1, width)
    positive = positive_ref[...]
    scores = score_scale * lax.dot_general(
        query, negs, (((1,), (1,)), ((), ())), preferred_element_type=f32
    )
    highest = jnp.maximum(jnp.max(scores, axis=1, keepdims=True), positive)
    total = jnp.exp(positive - highest) + jnp.sum(
        jnp.exp(scores - highest), axis=1, keepdims=True
    )
    log_total = highest + jnp.log(total)
    loss = log_total - positive
    step = loss_ref.shape[1]
    eye = lax.broadcasted_iota(i32, (step, step), 0) == lax.broadcasted_iota(i32, (step, step), 1)
    for line in range(loss_ref.shape[0]):
        part = loss[line * step : (line + 1) * step]
        loss_ref[line : line + 1, :] = jnp.sum(jnp.where(eye, part, 0.0), axis=0, keepdims=True)
    p_pos = jnp.exp(positive - log_total)
    p_neg_f = jnp.exp(scores - log_total)
    p_neg = p_neg_f.astype(bf16)
    gneg = score_scale * jnp.dot(p_neg_f.T.astype(bf16), query, preferred_element_type=f32)
    gneg_ref[...] = gneg.astype(bf16).reshape(gneg_ref.shape)
    grad_query = score_scale * (
        (p_pos - 1.0) * tails_f + jnp.dot(p_neg, negs, preferred_element_type=f32)
    )
    grads_ref[:trip] = (grad_query * scaling_ref[...] * (1.0 / bag)).astype(bf16)
    grads_ref[trip:] = (score_scale * (p_pos - 1.0) * query_f * (1.0 / bag)).astype(bf16)


def spread(counts_ref, grads_ref, gneg_ref, out_ref):
    bag = 16
    blocks, cap, half = out_ref.shape
    gneg = jnp.sum(gneg_ref[...].astype(f32), axis=0) * (1.0 / bag)
    grads = jnp.concatenate([grads_ref[...], gneg.astype(bf16)], axis=0)
    group = 8
    for first in range(0, blocks // 2, group):
        slot = jnp.dot(
            counts_ref[first * cap : (first + group) * cap, :], grads, preferred_element_type=f32
        ).astype(bf16)
        for s in range(group):
            for h in range(2):
                out_ref[2 * (first + s) + h] = slot[
                    s * cap : (s + 1) * cap, h * half : (h + 1) * half
                ]


def collect(turn, place_ref, asked_ref, grads_ref, out_ref, acc_ref):
    blocks, cap, half = grads_ref.shape
    chunk = acc_ref.shape[1] // 4
    parity = (place_ref[0] >> 1) & 1
    parity = 1 - parity if turn else parity
    lane = lax.broadcasted_iota(i32, (cap, 4 * chunk), 1)
    row = (lane + (lane // chunk + parity) * chunk).astype(i16)
    columns = asked_ref[...].T
    group = 8
    for first in range(0, blocks, group):
        picks = [
            ones_where(row == columns[:, b : b + 1].astype(i16))
            for b in range(first, first + group)
        ]
        part = jnp.dot(
            grads_ref[first : first + group].reshape(group * cap, half).T,
            jnp.concatenate(picks, axis=0),
            preferred_element_type=f32,
        )
        acc_ref[...] = part if first == 0 else acc_ref[...] + part
    for j in range(4):
        out_ref[j] = acc_ref[:, j * chunk : (j + 1) * chunk].T.astype(bf16)


def update(
    place_ref,
    table_ref,
    state_ref,
    own_ref,
    below_ref,
    above_ref,
    beyond_ref,
    table_out_ref,
    state_out_ref,
    sums_ref,
):
    half = own_ref.shape[2]
    chunk = own_ref.shape[1]
    kind = place_ref[0] & 3
    sums_ref[kind] = own_ref[...]
    sums_ref[(kind + 3) & 3] = below_ref[...]
    sums_ref[(kind + 1) & 3] = above_ref[...]
    sums_ref[(kind + 2) & 3] = beyond_ref[...]
    step = state_ref.shape[1]
    eye = lax.broadcasted_iota(i32, (step, step), 0) == lax.broadcasted_iota(i32, (step, step), 1)
    for c in range(8):
        at = 2 * (c % 2)
        whole = jnp.concatenate(
            [sums_ref[at, c // 2], sums_ref[at + 1, c // 2]], axis=1
        ).astype(f32)
        for q in range(chunk // step):
            gradient = whole[q * step : (q + 1) * step]
            line = c * (chunk // step) + q
            at = slice(line * step, (line + 1) * step)
            square = jnp.sum(gradient * gradient, axis=1, keepdims=True) * (1.0 / (2 * half))
            before = jnp.sum(
                jnp.where(eye, state_ref[line : line + 1, :], 0.0), axis=1, keepdims=True
            )
            fresh = before + square
            state_out_ref[line : line + 1, :] = jnp.sum(
                jnp.where(eye, fresh, 0.0), axis=0, keepdims=True
            )
            table_out_ref[at, :] = (
                table_ref[at, :].astype(f32) - learn_rate * gradient / jnp.sqrt(fresh)
            ).astype(bf16)


def on_device(
    feature_table,
    row_state,
    rel_diag,
    slot_rows,
    slot_counts,
    head_bags,
    tail_bags,
    negative_bags,
    relation_ids,
):
    n_feat = lax.axis_size("feat")
    n_dp = lax.axis_size("dp")
    cap = slot_rows.shape[2]
    rows, width = feature_table.shape
    trip = head_bags.shape[0]
    n_neg = negative_bags.shape[0]
    items = 2 * trip + n_neg
    slots = n_feat * cap
    half = width // 2
    place = lax.axis_index("dp").astype(i32).reshape(1)

    def shift(value, by):
        return lax.ppermute(value, "dp", [(i, (i + by) % n_dp) for i in range(n_dp)])

    pairs = [
        [f * n_dp + 2 * p + h for f in range(n_feat) for h in range(2)] for p in range(n_dp // 2)
    ]

    def across_pairs(value):
        return lax.all_to_all(
            value,
            ("feat", "dp"),
            split_axis=0,
            concat_axis=0,
            tiled=True,
            axis_index_groups=pairs,
        )

    place, slot_rows = lax.optimization_barrier((place, slot_rows))
    twice = jnp.broadcast_to(slot_rows[0][:, None], (n_feat, 2, cap)).reshape(2 * n_feat, cap)
    asked = across_pairs(twice)
    served = call(
        gather_rows,
        shape((n_feat, cap, width), bf16),
        [SM, VM, VM],
        flops=2 * slots * rows * width,
        moved=rows * width * 2 + slots * width * 2,
    )(place, asked, feature_table)
    fetched = lax.all_to_all(served, "feat", split_axis=0, concat_axis=0, tiled=True)
    fetched = fetched.reshape(slots, width)

    bags = jnp.concatenate([head_bags.T, tail_bags.T], axis=1)
    by_item, by_slot = call(
        count_entries,
        (shape((items, slots), bf16), shape((slots, items), bf16)),
        [SM, VM, VM],
        flops=8 * items * slots * 32,
        moved=4 * items * slots,
    )(slot_counts, bags, negative_bags)
    scaling = call(
        pick_relations,
        shape((trip, width), f32),
        [VM, VM],
        flops=2 * trip * rel_diag.shape[0] * width,
        moved=2 * rel_diag.shape[0] * width,
    )(relation_ids.reshape(trip // cap, cap), rel_diag)

    query, tails, positive, own_negs = call(
        pool,
        (
            shape((trip, width), bf16),
            shape((trip, width), bf16),
            shape((trip, 1), f32),
            shape((n_feat, n_neg, width), bf16),
        ),
        [pl.BlockSpec(memory_space=pl.ANY), VM, VM],
        scratch=[pltpu.VMEM((items, slots), bf16), pltpu.SemaphoreType.DMA((4,))],
        flops=2 * items * slots * width,
        moved=2 * slots * (width + items),
    )(by_item, fetched, scaling)
    negs = lax.all_to_all(own_negs, "feat", split_axis=0, concat_axis=0, tiled=True)
    loss, gneg, grads = call(
        score,
        (
            shape((trip // cap, cap), f32),
            shape((n_feat, n_neg, width), bf16),
            shape((2 * trip, width), bf16),
        ),
        [VM] * 5,
        limit=24,
        flops=6 * trip * n_feat * n_neg * width,
    )(query, tails, positive, scaling, negs)
    gneg = lax.all_to_all(gneg, "feat", split_axis=0, concat_axis=0, tiled=True)
    slot_grad = call(
        spread,
        shape((2 * n_feat, cap, half), bf16),
        [VM, VM, VM],
        limit=24,
        flops=2 * items * slots * width,
    )(by_slot, grads, gneg)
    arrived = across_pairs(slot_grad)
    chunk = rows // 8
    scratch = [pltpu.VMEM((half, 4 * chunk), f32)]
    sent = call(
        functools.partial(collect, 1),
        shape((4, chunk, half), bf16),
        [SM, VM, VM],
        scratch=scratch,
        flops=2 * slots * rows * half,
    )(place, asked, arrived)
    kept = call(
        functools.partial(collect, 0),
        shape((4, chunk, half), bf16),
        [SM, VM, VM],
        scratch=scratch,
        flops=2 * slots * rows * half,
        moved=2 * slots * width,
    )(place, asked, arrived)
    nearby = lax.ppermute(sent, "dp", [(i, i ^ 2) for i in range(n_dp)])
    kept = (kept.astype(f32) + nearby.astype(f32)).astype(bf16)
    apart = [[h + 4 * j for j in range(4)] for h in range(4)]
    quarter = lax.all_to_all(
        kept,
        "dp",
        split_axis=0,
        concat_axis=0,
        tiled=True,
        axis_index_groups=apart,
    )
    summed = jnp.sum(quarter.astype(f32), axis=0).astype(bf16)
    quad = lax.all_gather(summed, "dp", axis=0, axis_index_groups=apart)
    below, above = shift(quad, 1), shift(quad, -1)
    beyond = shift(quad, 2)
    new_table, new_state = call(
        update,
        (shape((rows, width), bf16), shape((rows // 128, 128), f32)),
        [SM] + [VM] * 6,
        scratch=[pltpu.VMEM((4, 4, chunk, half), bf16)],
    )(place, feature_table, row_state.reshape(rows // 128, 128), quad, below, above, beyond)
    return (loss.reshape(trip), new_table, new_state.reshape(rows))


def solution(mesh):
    in_specs = (
        P("feat", None),
        P("feat"),
        P(),
        P(("feat", "dp"), None, None),
        P(("feat", "dp"), None),
        P(("feat", "dp"), None),
        P(("feat", "dp"), None),
        P(("feat", "dp"), None),
        P(("feat", "dp")),
    )
    out_specs = (P(("feat", "dp")), P("feat", None), P("feat"))
    return jax.shard_map(
        on_device, mesh=mesh, in_specs=in_specs, out_specs=out_specs, check_vma=False
    )
```

```python
import functools

import jax
import jax.numpy as jnp
from jax import lax
from jax.experimental import pallas as pl
from jax.experimental.pallas import tpu as pltpu
from jax.sharding import PartitionSpec as P

score_scale = 4.0
learn_rate = 0.1
f32 = jnp.float32
bf16 = jnp.bfloat16
i32 = jnp.int32
i16 = jnp.int16

VM = pl.BlockSpec(memory_space=pltpu.VMEM)
SM = pl.BlockSpec(memory_space=pltpu.SMEM)
ANY = pl.BlockSpec(memory_space=pl.ANY)
MIB = 1 << 20
LIMIT = 48


def call(body, out_shape, in_specs, outs=None, scratch=(), flops=0, moved=0, limit=LIMIT):
    outs = jax.tree.map(lambda _: VM, out_shape) if outs is None else outs
    return pl.pallas_call(
        body,
        out_shape=out_shape,
        in_specs=in_specs,
        out_specs=outs,
        scratch_shapes=list(scratch),
        compiler_params=pltpu.CompilerParams(vmem_limit_bytes=limit * MIB),
        cost_estimate=pl.CostEstimate(flops=flops, bytes_accessed=moved, transcendentals=0),
    )


def shape(dims, dtype):
    return jax.ShapeDtypeStruct(dims, dtype)


def ones_where(mask):
    return jnp.where(mask, jnp.ones((), bf16), jnp.zeros((), bf16))


def narrow_iota(dims, axis):
    return lax.broadcasted_iota(i32, dims, axis).astype(i16)


def gather_rows(place_ref, asked_ref, table_ref, out_ref, held_ref, sems):
    sources, cap, width = held_ref.shape
    even = (place_ref[0] & 1) == 0
    columns = asked_ref[...].T
    lanes = narrow_iota((cap, table_ref.shape[0]), 1)
    group = sources // sems.shape[0]
    copies = []
    for k in range(sems.shape[0]):
        span = slice(k * group, (k + 1) * group)
        picks = []
        for s in range(k * group, (k + 1) * group):
            column = jnp.where(
                even, columns[:, 2 * s : 2 * s + 1], columns[:, 2 * s + 1 : 2 * s + 2]
            )
            picks.append(ones_where(lanes == column.astype(i16)))
        got = jnp.dot(jnp.concatenate(picks, axis=0), table_ref[...], preferred_element_type=f32)
        held_ref[span] = got.astype(bf16).reshape(group, cap, width)
        copies.append(pltpu.make_async_copy(held_ref.at[span], out_ref.at[span], sems.at[k]))
        copies[-1].start()
    for copy in copies:
        copy.wait()


def count_entries(counts_ref, bags_ref, neg_ref, by_item_ref, by_slot_ref):
    bag, trips = bags_ref.shape
    negs = neg_ref.shape[0]
    owners = counts_ref.shape[1]
    cap = by_slot_ref.shape[0] // owners
    sub_at = lax.broadcasted_iota(i32, (cap, 1), 0)
    lane_at = lax.broadcasted_iota(i32, (1, cap), 1)
    sub = narrow_iota((cap, cap), 0)
    for first in range(0, trips, cap):
        span = slice(first, first + cap)
        entries = [bags_ref[b : b + 1, span].astype(i16) for b in range(bag)]

        def step(pair, carry):
            for owner in (2 * pair, 2 * pair + 1):
                at = pl.ds(pl.multiple_of(owner * cap, cap), cap)
                here = sub + (owner * cap).astype(i16)
                total = ones_where(here == entries[0])
                for b in range(1, bag):
                    total = total + ones_where(here == entries[b])
                total = total * jnp.where(sub_at < counts_ref[0, owner], 1.0, 0.0).astype(bf16)
                by_slot_ref[at, span] = total
                by_item_ref[span, at] = total.T
            return carry

        lax.fori_loop(0, owners // 2, step, 0)

    lane = narrow_iota((negs, cap), 1)
    columns = [
        jnp.broadcast_to(neg_ref[:, b : b + 1], (negs, cap)).astype(i16) for b in range(bag)
    ]
    span = slice(trips, trips + negs)

    def last(owner, carry):
        at = pl.ds(pl.multiple_of(owner * cap, cap), cap)
        here = lane + (owner * cap).astype(i16)
        total = ones_where(here == columns[0])
        for b in range(1, bag):
            total = total + ones_where(here == columns[b])
        total = total * jnp.where(lane_at < counts_ref[0, owner], 1.0, 0.0).astype(bf16)
        by_item_ref[span, at] = total
        by_slot_ref[at, span] = total.T
        return carry

    lax.fori_loop(0, owners, last, 0)


def pick_relations(ids_ref, rel_ref, out_ref):
    step = ids_ref.shape[1]
    relations = rel_ref.shape[0]
    eye = lax.broadcasted_iota(i32, (step, step), 0) == lax.broadcasted_iota(i32, (step, step), 1)
    lanes = narrow_iota((step, relations), 1)
    for line in range(ids_ref.shape[0]):
        column = jnp.sum(jnp.where(eye, ids_ref[line : line + 1, :], 0), axis=1, keepdims=True)
        pick = ones_where(lanes == column.astype(i16))
        out_ref[line * step : (line + 1) * step, :] = jnp.dot(
            pick, rel_ref[...], preferred_element_type=f32
        )


def pool(counts_ref, fetched_ref, scaling_ref, query_ref, tails_ref, positive_ref, negs_ref):
    bag = 16
    trip = query_ref.shape[0]
    pooled = jnp.dot(counts_ref[...], fetched_ref[...], preferred_element_type=f32)
    entity = (pooled * (1.0 / bag)).astype(bf16)
    negs_ref[...] = jnp.broadcast_to(entity[None, 2 * trip :], negs_ref.shape)
    tails = entity[trip : 2 * trip]
    query = (entity[:trip].astype(f32) * scaling_ref[...]).astype(bf16)
    query_ref[...] = query
    tails_ref[...] = tails
    positive_ref[...] = score_scale * jnp.sum(
        query.astype(f32) * tails.astype(f32), axis=1, keepdims=True
    )


def score(query_ref, tails_ref, positive_ref, scaling_ref, negs_ref, loss_ref, gneg_ref, grads_ref):
    bag = 16
    trip, width = query_ref.shape
    query = query_ref[...]
    query_f = query.astype(f32)
    tails_f = tails_ref[...].astype(f32)
    negs = negs_ref[...].reshape(-1, width)
    positive = positive_ref[...]
    scores = score_scale * lax.dot_general(
        query, negs, (((1,), (1,)), ((), ())), preferred_element_type=f32
    )
    highest = jnp.maximum(jnp.max(scores, axis=1, keepdims=True), positive)
    total = jnp.exp(positive - highest) + jnp.sum(
        jnp.exp(scores - highest), axis=1, keepdims=True
    )
    log_total = highest + jnp.log(total)
    loss = log_total - positive
    step = loss_ref.shape[1]
    eye = lax.broadcasted_iota(i32, (step, step), 0) == lax.broadcasted_iota(i32, (step, step), 1)
    for line in range(loss_ref.shape[0]):
        part = loss[line * step : (line + 1) * step]
        loss_ref[line : line + 1, :] = jnp.sum(jnp.where(eye, part, 0.0), axis=0, keepdims=True)
    p_pos = jnp.exp(positive - log_total)
    p_neg_f = jnp.exp(scores - log_total)
    p_neg = p_neg_f.astype(bf16)
    gneg = score_scale * jnp.dot(p_neg_f.T.astype(bf16), query, preferred_element_type=f32)
    gneg_ref[...] = gneg.astype(bf16).reshape(gneg_ref.shape)
    grad_query = score_scale * (
        (p_pos - 1.0) * tails_f + jnp.dot(p_neg, negs, preferred_element_type=f32)
    )
    grads_ref[:trip] = (grad_query * scaling_ref[...] * (1.0 / bag)).astype(bf16)
    grads_ref[trip:] = (score_scale * (p_pos - 1.0) * query_f * (1.0 / bag)).astype(bf16)


def spread(counts_ref, grads_ref, gneg_ref, out_ref):
    bag = 16
    blocks, cap, half = out_ref.shape
    gneg = jnp.sum(gneg_ref[...].astype(f32), axis=0) * (1.0 / bag)
    grads = jnp.concatenate([grads_ref[...], gneg.astype(bf16)], axis=0)
    group = 8
    for first in range(0, blocks // 2, group):
        slot = jnp.dot(
            counts_ref[first * cap : (first + group) * cap, :], grads, preferred_element_type=f32
        ).astype(bf16)
        for s in range(group):
            for h in range(2):
                out_ref[2 * (first + s) + h] = slot[
                    s * cap : (s + 1) * cap, h * half : (h + 1) * half
                ]


def collect(turn, place_ref, asked_ref, grads_ref, *refs):
    out_refs, acc_ref = refs[:-1], refs[-1]
    blocks, cap, half = grads_ref.shape
    chunk = acc_ref.shape[1] // 4
    parity = (place_ref[0] >> 1) & 1
    parity = 1 - parity if turn else parity
    lane = lax.broadcasted_iota(i32, (cap, 4 * chunk), 1)
    row = (lane + (lane // chunk + parity) * chunk).astype(i16)
    columns = asked_ref[...].T
    group = 8
    for first in range(0, blocks, group):
        picks = [
            ones_where(row == columns[:, b : b + 1].astype(i16))
            for b in range(first, first + group)
        ]
        part = jnp.dot(
            grads_ref[first : first + group].reshape(group * cap, half).T,
            jnp.concatenate(picks, axis=0),
            preferred_element_type=f32,
        )
        acc_ref[...] = part if first == 0 else acc_ref[...] + part
    j = 0
    for ref in out_refs:
        for k in range(ref.shape[0]):
            ref[k] = acc_ref[:, j * chunk : (j + 1) * chunk].T.astype(bf16)
            j += 1


def update(
    place_ref,
    table_ref,
    state_ref,
    own_ref,
    below_ref,
    above_ref,
    low_ref,
    high_ref,
    table_out_ref,
    state_out_ref,
    sums_ref,
    fresh_ref,
    sems,
):
    half = own_ref.shape[2]
    chunk = own_ref.shape[1]
    kind = place_ref[0] & 3
    sums_ref[kind] = own_ref[...]
    sums_ref[(kind + 3) & 3] = below_ref[...]
    sums_ref[(kind + 1) & 3] = above_ref[...]
    sums_ref[(kind + 2) & 3, :2] = low_ref[...]
    sums_ref[(kind + 2) & 3, 2:] = high_ref[...]
    step = state_ref.shape[1]
    eye = lax.broadcasted_iota(i32, (step, step), 0) == lax.broadcasted_iota(i32, (step, step), 1)
    copies = []
    for c in range(8):
        at = 2 * (c % 2)
        whole = jnp.concatenate(
            [sums_ref[at, c // 2], sums_ref[at + 1, c // 2]], axis=1
        ).astype(f32)
        for q in range(chunk // step):
            gradient = whole[q * step : (q + 1) * step]
            line = c * (chunk // step) + q
            at = slice(line * step, (line + 1) * step)
            square = jnp.sum(gradient * gradient, axis=1, keepdims=True) * (1.0 / (2 * half))
            before = jnp.sum(
                jnp.where(eye, state_ref[line : line + 1, :], 0.0), axis=1, keepdims=True
            )
            fresh = before + square
            state_out_ref[line : line + 1, :] = jnp.sum(
                jnp.where(eye, fresh, 0.0), axis=0, keepdims=True
            )
            fresh_ref[at, :] = (
                table_ref[at, :].astype(f32) - learn_rate * gradient / jnp.sqrt(fresh)
            ).astype(bf16)
        span = pl.ds(c * chunk, chunk)
        copies.append(
            pltpu.make_async_copy(fresh_ref.at[span, :], table_out_ref.at[span, :], sems.at[c])
        )
        copies[-1].start()
    for copy in copies:
        copy.wait()


def on_device(
    feature_table,
    row_state,
    rel_diag,
    slot_rows,
    slot_counts,
    head_bags,
    tail_bags,
    negative_bags,
    relation_ids,
):
    n_feat = lax.axis_size("feat")
    n_dp = lax.axis_size("dp")
    cap = slot_rows.shape[2]
    rows, width = feature_table.shape
    trip = head_bags.shape[0]
    n_neg = negative_bags.shape[0]
    items = 2 * trip + n_neg
    slots = n_feat * cap
    half = width // 2
    place = lax.axis_index("dp").astype(i32).reshape(1)

    def shift(value, by):
        return lax.ppermute(value, "dp", [(i, (i + by) % n_dp) for i in range(n_dp)])

    pairs = [
        [f * n_dp + 2 * p + h for f in range(n_feat) for h in range(2)] for p in range(n_dp // 2)
    ]

    def across_pairs(value):
        return lax.all_to_all(
            value,
            ("feat", "dp"),
            split_axis=0,
            concat_axis=0,
            tiled=True,
            axis_index_groups=pairs,
        )

    place, slot_rows = lax.optimization_barrier((place, slot_rows))
    twice = jnp.broadcast_to(slot_rows[0][:, None], (n_feat, 2, cap)).reshape(2 * n_feat, cap)
    asked = across_pairs(twice)
    served = call(
        gather_rows,
        shape((n_feat, cap, width), bf16),
        [SM, VM, VM],
        outs=ANY,
        scratch=[pltpu.VMEM((n_feat, cap, width), bf16), pltpu.SemaphoreType.DMA((8,))],
        limit=60,
        flops=2 * slots * rows * width,
        moved=rows * width * 2 + slots * width * 2,
    )(place, asked, feature_table)
    fetched = lax.all_to_all(served, "feat", split_axis=0, concat_axis=0, tiled=True)
    fetched = fetched.reshape(slots, width)

    bags = jnp.concatenate([head_bags.T, tail_bags.T], axis=1)
    by_item, by_slot = call(
        count_entries,
        (shape((items, slots), bf16), shape((slots, items), bf16)),
        [SM, VM, VM],
        flops=8 * items * slots * 32,
        moved=4 * items * slots,
    )(slot_counts, bags, negative_bags)
    scaling = call(
        pick_relations,
        shape((trip, width), f32),
        [VM, VM],
        flops=2 * trip * rel_diag.shape[0] * width,
        moved=2 * rel_diag.shape[0] * width,
    )(relation_ids.reshape(trip // cap, cap), rel_diag)

    query, tails, positive, own_negs = call(
        pool,
        (
            shape((trip, width), bf16),
            shape((trip, width), bf16),
            shape((trip, 1), f32),
            shape((n_feat, n_neg, width), bf16),
        ),
        [VM, VM, VM],
        flops=2 * items * slots * width,
        moved=2 * slots * (width + items),
    )(by_item, fetched, scaling)
    negs = lax.all_to_all(own_negs, "feat", split_axis=0, concat_axis=0, tiled=True)
    loss, gneg, grads = call(
        score,
        (
            shape((trip // cap, cap), f32),
            shape((n_feat, n_neg, width), bf16),
            shape((2 * trip, width), bf16),
        ),
        [VM] * 5,
        limit=24,
        flops=6 * trip * n_feat * n_neg * width,
    )(query, tails, positive, scaling, negs)
    gneg = lax.all_to_all(gneg, "feat", split_axis=0, concat_axis=0, tiled=True)
    slot_grad = call(
        spread,
        shape((2 * n_feat, cap, half), bf16),
        [VM, VM, VM],
        limit=24,
        flops=2 * items * slots * width,
    )(by_slot, grads, gneg)
    arrived = across_pairs(slot_grad)
    chunk = rows // 8
    scratch = [pltpu.VMEM((half, 4 * chunk), f32)]
    up, down = call(
        functools.partial(collect, 1),
        (shape((2, chunk, half), bf16), shape((2, chunk, half), bf16)),
        [SM, VM, VM],
        scratch=scratch,
        flops=2 * slots * rows * half,
    )(place, asked, arrived)
    kept = call(
        functools.partial(collect, 0),
        shape((4, chunk, half), bf16),
        [SM, VM, VM],
        scratch=scratch,
        flops=2 * slots * rows * half,
        moved=2 * slots * width,
    )(place, asked, arrived)
    nearby = jnp.concatenate([shift(up, 2), shift(down, -2)], axis=0)
    kept = (kept.astype(f32) + nearby.astype(f32)).astype(bf16)
    apart = [[h + 4 * j for j in range(4)] for h in range(4)]
    quarter = lax.all_to_all(
        kept,
        "dp",
        split_axis=0,
        concat_axis=0,
        tiled=True,
        axis_index_groups=apart,
    )
    summed = jnp.sum(quarter.astype(f32), axis=0).astype(bf16)
    quad = lax.all_gather(summed, "dp", axis=0, axis_index_groups=apart)
    below, above = shift(quad, 1), shift(quad, -1)
    low, high = shift(quad[:2], 2), shift(quad[2:], -2)
    new_table, new_state = call(
        update,
        (shape((rows, width), bf16), shape((rows // 128, 128), f32)),
        [SM] + [VM] * 7,
        outs=(ANY, VM),
        scratch=[
            pltpu.VMEM((4, 4, chunk, half), bf16),
            pltpu.VMEM((rows, width), bf16),
            pltpu.SemaphoreType.DMA((8,)),
        ],
    )(place, feature_table, row_state.reshape(rows // 128, 128), quad, below, above, low, high)
    return (loss.reshape(trip), new_table, new_state.reshape(rows))


def solution(mesh):
    in_specs = (
        P("feat", None),
        P("feat"),
        P(),
        P(("feat", "dp"), None, None),
        P(("feat", "dp"), None),
        P(("feat", "dp"), None),
        P(("feat", "dp"), None),
        P(("feat", "dp"), None),
        P(("feat", "dp")),
    )
    out_specs = (P(("feat", "dp")), P("feat", None), P("feat"))
    return jax.shard_map(
        on_device, mesh=mesh, in_specs=in_specs, out_specs=out_specs, check_vma=False
    )
```

```python
import functools

import jax
import jax.numpy as jnp
from jax import lax
from jax.experimental import pallas as pl
from jax.experimental.pallas import tpu as pltpu
from jax.sharding import PartitionSpec as P

score_scale = 4.0
learn_rate = 0.1
f32 = jnp.float32
bf16 = jnp.bfloat16
i32 = jnp.int32
i16 = jnp.int16

VM = pl.BlockSpec(memory_space=pltpu.VMEM)
SM = pl.BlockSpec(memory_space=pltpu.SMEM)
ANY = pl.BlockSpec(memory_space=pl.ANY)
MIB = 1 << 20
LIMIT = 48


def call(body, out_shape, in_specs, outs=None, scratch=(), flops=0, moved=0, limit=LIMIT):
    outs = jax.tree.map(lambda _: VM, out_shape) if outs is None else outs
    return pl.pallas_call(
        body,
        out_shape=out_shape,
        in_specs=in_specs,
        out_specs=outs,
        scratch_shapes=list(scratch),
        compiler_params=pltpu.CompilerParams(vmem_limit_bytes=limit * MIB),
        cost_estimate=pl.CostEstimate(flops=flops, bytes_accessed=moved, transcendentals=0),
    )


def shape(dims, dtype):
    return jax.ShapeDtypeStruct(dims, dtype)


def ones_where(mask):
    return jnp.where(mask, jnp.ones((), bf16), jnp.zeros((), bf16))


def narrow_iota(dims, axis):
    return lax.broadcasted_iota(i32, dims, axis).astype(i16)


def gather_rows(asked_ref, table_ref, out_ref):
    sources, cap, width = out_ref.shape
    columns = asked_ref[...].T
    lanes = narrow_iota((cap, table_ref.shape[0]), 1)
    group = 8
    for first in range(0, sources, group):
        picks = [
            ones_where(lanes == columns[:, s : s + 1].astype(i16))
            for s in range(first, first + group)
        ]
        got = jnp.dot(jnp.concatenate(picks, axis=0), table_ref[...], preferred_element_type=f32)
        out_ref[first : first + group] = got.astype(bf16).reshape(group, cap, width)


def count_entries(counts_ref, bags_ref, neg_ref, by_item_ref, by_slot_ref):
    bag, trips = bags_ref.shape
    negs = neg_ref.shape[0]
    owners = counts_ref.shape[1]
    cap = by_slot_ref.shape[0] // owners
    sub_at = lax.broadcasted_iota(i32, (cap, 1), 0)
    lane_at = lax.broadcasted_iota(i32, (1, cap), 1)
    sub = narrow_iota((cap, cap), 0)
    for first in range(0, trips, cap):
        span = slice(first, first + cap)
        entries = [bags_ref[b : b + 1, span].astype(i16) for b in range(bag)]

        def step(pair, carry):
            for owner in (2 * pair, 2 * pair + 1):
                at = pl.ds(pl.multiple_of(owner * cap, cap), cap)
                here = sub + (owner * cap).astype(i16)
                total = ones_where(here == entries[0])
                for b in range(1, bag):
                    total = total + ones_where(here == entries[b])
                total = total * jnp.where(sub_at < counts_ref[0, owner], 1.0, 0.0).astype(bf16)
                by_slot_ref[at, span] = total
                by_item_ref[span, at] = total.T
            return carry

        lax.fori_loop(0, owners // 2, step, 0)

    lane = narrow_iota((negs, cap), 1)
    columns = [
        jnp.broadcast_to(neg_ref[:, b : b + 1], (negs, cap)).astype(i16) for b in range(bag)
    ]
    span = slice(trips, trips + negs)

    def last(owner, carry):
        at = pl.ds(pl.multiple_of(owner * cap, cap), cap)
        here = lane + (owner * cap).astype(i16)
        total = ones_where(here == columns[0])
        for b in range(1, bag):
            total = total + ones_where(here == columns[b])
        total = total * jnp.where(lane_at < counts_ref[0, owner], 1.0, 0.0).astype(bf16)
        by_item_ref[span, at] = total
        by_slot_ref[at, span] = total.T
        return carry

    lax.fori_loop(0, owners, last, 0)


def pick_relations(ids_ref, rel_ref, out_ref):
    step = ids_ref.shape[1]
    relations = rel_ref.shape[0]
    eye = lax.broadcasted_iota(i32, (step, step), 0) == lax.broadcasted_iota(i32, (step, step), 1)
    lanes = narrow_iota((step, relations), 1)
    for line in range(ids_ref.shape[0]):
        column = jnp.sum(jnp.where(eye, ids_ref[line : line + 1, :], 0), axis=1, keepdims=True)
        pick = ones_where(lanes == column.astype(i16))
        out_ref[line * step : (line + 1) * step, :] = jnp.dot(
            pick, rel_ref[...], preferred_element_type=f32
        )


def pool(counts_ref, fetched_ref, scaling_ref, _, query_ref, tails_ref, positive_ref, negs_ref):
    bag = 16
    trip = query_ref.shape[0]
    pooled = jnp.dot(counts_ref[...], fetched_ref[...], preferred_element_type=f32)
    entity = (pooled * (1.0 / bag)).astype(bf16)
    negs_ref[...] = jnp.broadcast_to(entity[None, 2 * trip :], negs_ref.shape)
    tails = entity[trip : 2 * trip]
    query = (entity[:trip].astype(f32) * scaling_ref[...]).astype(bf16)
    query_ref[...] = query
    tails_ref[...] = tails
    positive_ref[...] = score_scale * jnp.sum(
        query.astype(f32) * tails.astype(f32), axis=1, keepdims=True
    )


def score(query_ref, tails_ref, positive_ref, scaling_ref, negs_ref, loss_ref, gneg_ref, grads_ref):
    bag = 16
    trip, width = query_ref.shape
    query = query_ref[...]
    query_f = query.astype(f32)
    tails_f = tails_ref[...].astype(f32)
    negs = negs_ref[...].reshape(-1, width)
    positive = positive_ref[...]
    scores = score_scale * lax.dot_general(
        query, negs, (((1,), (1,)), ((), ())), preferred_element_type=f32
    )
    highest = jnp.maximum(jnp.max(scores, axis=1, keepdims=True), positive)
    total = jnp.exp(positive - highest) + jnp.sum(
        jnp.exp(scores - highest), axis=1, keepdims=True
    )
    log_total = highest + jnp.log(total)
    loss = log_total - positive
    step = loss_ref.shape[1]
    eye = lax.broadcasted_iota(i32, (step, step), 0) == lax.broadcasted_iota(i32, (step, step), 1)
    for line in range(loss_ref.shape[0]):
        part = loss[line * step : (line + 1) * step]
        loss_ref[line : line + 1, :] = jnp.sum(jnp.where(eye, part, 0.0), axis=0, keepdims=True)
    p_pos = jnp.exp(positive - log_total)
    p_neg_f = jnp.exp(scores - log_total)
    p_neg = p_neg_f.astype(bf16)
    gneg = score_scale * jnp.dot(p_neg_f.T.astype(bf16), query, preferred_element_type=f32)
    gneg_ref[...] = gneg.astype(bf16).reshape(gneg_ref.shape)
    grad_query = score_scale * (
        (p_pos - 1.0) * tails_f + jnp.dot(p_neg, negs, preferred_element_type=f32)
    )
    grads_ref[:trip] = (grad_query * scaling_ref[...] * (1.0 / bag)).astype(bf16)
    grads_ref[trip:] = (score_scale * (p_pos - 1.0) * query_f * (1.0 / bag)).astype(bf16)


def spread(counts_ref, grads_ref, gneg_ref, out_ref, held_ref, sems):
    bag = 16
    blocks, cap, half = out_ref.shape
    pieces = sems.shape[0]
    group = blocks // 2 // pieces
    spans = [pl.ds(k * group * cap, group * cap) for k in range(pieces)]
    copies = [
        pltpu.make_async_copy(counts_ref.at[span, :], held_ref.at[span, :], sems.at[k])
        for k, span in enumerate(spans)
    ]
    for copy in copies:
        copy.start()
    gneg = jnp.sum(gneg_ref[...].astype(f32), axis=0) * (1.0 / bag)
    grads = jnp.concatenate([grads_ref[...], gneg.astype(bf16)], axis=0)
    for k, (copy, span) in enumerate(zip(copies, spans)):
        copy.wait()
        slot = jnp.dot(held_ref[span, :], grads, preferred_element_type=f32).astype(bf16)
        for s in range(group):
            for h in range(2):
                out_ref[2 * (k * group + s) + h] = slot[
                    s * cap : (s + 1) * cap, h * half : (h + 1) * half
                ]


def collect(turn, place_ref, own_ref, other_ref, grads_ref, *refs):
    out_refs, acc_ref = refs[:-1], refs[-1]
    blocks, cap, half = grads_ref.shape
    chunk = acc_ref.shape[1] // 4
    parity = (place_ref[0] >> 1) & 1
    parity = 1 - parity if turn else parity
    lane = lax.broadcasted_iota(i32, (cap, 4 * chunk), 1)
    row = (lane + (lane // chunk + parity) * chunk).astype(i16)
    even = (place_ref[0] & 1) == 0
    own, other = own_ref[...].T, other_ref[...].T
    columns = (jnp.where(even, own, other), jnp.where(even, other, own))
    group = 8
    for first in range(0, blocks, group):
        picks = [
            ones_where(row == columns[b % 2][:, b // 2 : b // 2 + 1].astype(i16))
            for b in range(first, first + group)
        ]
        part = jnp.dot(
            grads_ref[first : first + group].reshape(group * cap, half).T,
            jnp.concatenate(picks, axis=0),
            preferred_element_type=f32,
        )
        acc_ref[...] = part if first == 0 else acc_ref[...] + part
    j = 0
    for ref in out_refs:
        for k in range(ref.shape[0]):
            ref[k] = acc_ref[:, j * chunk : (j + 1) * chunk].T.astype(bf16)
            j += 1


def update(
    place_ref,
    table_ref,
    state_ref,
    own_ref,
    below_ref,
    above_ref,
    low_ref,
    high_ref,
    table_out_ref,
    state_out_ref,
    sums_ref,
):
    half = own_ref.shape[2]
    chunk = own_ref.shape[1]
    kind = place_ref[0] & 3
    sums_ref[kind] = own_ref[...]
    sums_ref[(kind + 3) & 3] = below_ref[...]
    sums_ref[(kind + 1) & 3] = above_ref[...]
    sums_ref[(kind + 2) & 3, :2] = low_ref[...]
    sums_ref[(kind + 2) & 3, 2:] = high_ref[...]
    step = state_ref.shape[1]
    eye = lax.broadcasted_iota(i32, (step, step), 0) == lax.broadcasted_iota(i32, (step, step), 1)
    for c in range(8):
        at = 2 * (c % 2)
        whole = jnp.concatenate(
            [sums_ref[at, c // 2], sums_ref[at + 1, c // 2]], axis=1
        ).astype(f32)
        for q in range(chunk // step):
            gradient = whole[q * step : (q + 1) * step]
            line = c * (chunk // step) + q
            at = slice(line * step, (line + 1) * step)
            square = jnp.sum(gradient * gradient, axis=1, keepdims=True) * (1.0 / (2 * half))
            before = jnp.sum(
                jnp.where(eye, state_ref[line : line + 1, :], 0.0), axis=1, keepdims=True
            )
            fresh = before + square
            state_out_ref[line : line + 1, :] = jnp.sum(
                jnp.where(eye, fresh, 0.0), axis=0, keepdims=True
            )
            table_out_ref[at, :] = (
                table_ref[at, :].astype(f32) - learn_rate * gradient / jnp.sqrt(fresh)
            ).astype(bf16)


def on_device(
    feature_table,
    row_state,
    rel_diag,
    slot_rows,
    slot_counts,
    head_bags,
    tail_bags,
    negative_bags,
    relation_ids,
):
    n_feat = lax.axis_size("feat")
    n_dp = lax.axis_size("dp")
    cap = slot_rows.shape[2]
    rows, width = feature_table.shape
    trip = head_bags.shape[0]
    n_neg = negative_bags.shape[0]
    items = 2 * trip + n_neg
    slots = n_feat * cap
    half = width // 2
    place = lax.axis_index("dp").astype(i32).reshape(1)

    def shift(value, by):
        return lax.ppermute(value, "dp", [(i, (i + by) % n_dp) for i in range(n_dp)])

    pairs = [
        [f * n_dp + 2 * p + h for f in range(n_feat) for h in range(2)] for p in range(n_dp // 2)
    ]

    place, slot_rows = lax.optimization_barrier((place, slot_rows))
    asked = lax.all_to_all(slot_rows[0], "feat", split_axis=0, concat_axis=0, tiled=True)
    asked_other = lax.ppermute(asked, "dp", [(i, i ^ 1) for i in range(n_dp)])
    served = call(
        gather_rows,
        shape((n_feat, cap, width), bf16),
        [VM, VM],
        flops=2 * slots * rows * width,
        moved=rows * width * 2 + slots * width * 2,
    )(asked, feature_table)
    fetched = lax.all_to_all(served, "feat", split_axis=0, concat_axis=0, tiled=True)
    fetched = fetched.reshape(slots, width)

    bags = jnp.concatenate([head_bags.T, tail_bags.T], axis=1)
    by_item, by_slot = call(
        count_entries,
        (shape((items, slots), bf16), shape((slots, items), bf16)),
        [SM, VM, VM],
        flops=8 * items * slots * 32,
        moved=4 * items * slots,
    )(slot_counts, bags, negative_bags)
    scaling = call(
        pick_relations,
        shape((trip, width), f32),
        [VM, VM],
        flops=2 * trip * rel_diag.shape[0] * width,
        moved=2 * rel_diag.shape[0] * width,
    )(relation_ids.reshape(trip // cap, cap), rel_diag)

    query, tails, positive, own_negs = call(
        pool,
        (
            shape((trip, width), bf16),
            shape((trip, width), bf16),
            shape((trip, 1), f32),
            shape((n_feat, n_neg, width), bf16),
        ),
        [VM, VM, VM, ANY],
        flops=2 * items * slots * width,
        moved=2 * slots * (width + items),
    )(by_item, fetched, scaling, asked_other)
    negs = lax.all_to_all(own_negs, "feat", split_axis=0, concat_axis=0, tiled=True)
    loss, gneg, grads = call(
        score,
        (
            shape((trip // cap, cap), f32),
            shape((n_feat, n_neg, width), bf16),
            shape((2 * trip, width), bf16),
        ),
        [VM] * 5,
        limit=24,
        flops=6 * trip * n_feat * n_neg * width,
    )(query, tails, positive, scaling, negs)
    gneg = lax.all_to_all(gneg, "feat", split_axis=0, concat_axis=0, tiled=True)
    slot_grad = call(
        spread,
        shape((2 * n_feat, cap, half), bf16),
        [ANY, VM, VM],
        scratch=[pltpu.VMEM((slots, items), bf16), pltpu.SemaphoreType.DMA((8,))],
        flops=2 * items * slots * width,
    )(by_slot, grads, gneg)
    arrived = lax.all_to_all(
        slot_grad,
        ("feat", "dp"),
        split_axis=0,
        concat_axis=0,
        tiled=True,
        axis_index_groups=pairs,
    )
    chunk = rows // 8
    scratch = [pltpu.VMEM((half, 4 * chunk), f32)]
    up, down = call(
        functools.partial(collect, 1),
        (shape((2, chunk, half), bf16), shape((2, chunk, half), bf16)),
        [SM, VM, VM, VM],
        scratch=scratch,
        flops=2 * slots * rows * half,
    )(place, asked, asked_other, arrived)
    kept = call(
        functools.partial(collect, 0),
        shape((4, chunk, half), bf16),
        [SM, VM, VM, VM],
        scratch=scratch,
        flops=2 * slots * rows * half,
        moved=2 * slots * width,
    )(place, asked, asked_other, arrived)
    nearby = jnp.concatenate([shift(up, 2), shift(down, -2)], axis=0)
    kept = (kept.astype(f32) + nearby.astype(f32)).astype(bf16)
    apart = [[h + 4 * j for j in range(4)] for h in range(4)]
    quarter = lax.all_to_all(
        kept,
        "dp",
        split_axis=0,
        concat_axis=0,
        tiled=True,
        axis_index_groups=apart,
    )
    summed = jnp.sum(quarter.astype(f32), axis=0).astype(bf16)
    quad = lax.all_gather(summed, "dp", axis=0, axis_index_groups=apart)
    below, above = shift(quad, 1), shift(quad, -1)
    low, high = shift(quad[:2], 2), shift(quad[2:], -2)
    new_table, new_state = call(
        update,
        (shape((rows, width), bf16), shape((rows // 128, 128), f32)),
        [SM] + [VM] * 7,
        scratch=[pltpu.VMEM((4, 4, chunk, half), bf16)],
    )(place, feature_table, row_state.reshape(rows // 128, 128), quad, below, above, low, high)
    return (loss.reshape(trip), new_table, new_state.reshape(rows))


def solution(mesh):
    in_specs = (
        P("feat", None),
        P("feat"),
        P(),
        P(("feat", "dp"), None, None),
        P(("feat", "dp"), None),
        P(("feat", "dp"), None),
        P(("feat", "dp"), None),
        P(("feat", "dp"), None),
        P(("feat", "dp")),
    )
    out_specs = (P(("feat", "dp")), P("feat", None), P("feat"))
    return jax.shard_map(
        on_device, mesh=mesh, in_specs=in_specs, out_specs=out_specs, check_vma=False
    )
```
